256 devices in a mesh: gx: 4 (over x), gy: 8 (over z_hi, core), gz: 8 (over z_lo, y).
Axes of the slice: x: 4, y: 4, z: 8 (z_hi: 4, z_lo: 2; z = z_hi * 2 + z_lo), core: 2. Of those that a mesh axis runs over, the one named last changes fastest.
Arguments:
- latent: float32 [3, 64, 128, 512], P(None, 'gy', 'gz', 'gx'), may hold values from -6 to 6
- cotangent: float32 [3, 64, 128, 512], P(None, 'gy', 'gz', 'gx'), may hold values from -6 to 6
Outputs:
- moved: float32 [3, 64, 128, 512], P(None, 'gy', 'gz', 'gx')
- grad_latent: float32 [3, 64, 128, 512], P(None, 'gy', 'gz', 'gx')
The draws below stay inside these ranges and needn't reach their ends.
All inputs are finite; a program needn't handle non-finite values.
Results may differ from the reference program's by a relative error of at most 0.0003.
Values sent between devices are 32-bit elements; how exact they have to be, the bound alone decides.
A program may use at most 128 MiB of HBM per device.

```python
import math
import jax
import jax.numpy as jnp

FACTOR = 2
NX = 64
NY = 128
NZ = 512


def shard_levels(key, extent, cuts, low, high):
    def one(position, shards_of):
        steps = jax.random.uniform(jax.random.fold_in(jax.random.fold_in(key, 6), position), (shards_of,), jnp.float32, low / len(cuts), high / len(cuts))
        return jnp.repeat(jnp.exp(steps), extent[position] // shards_of).reshape((-1,) + (1,) * (len(extent) - position - 1))

    factor_of = one(*cuts[0])
    for cut in cuts[1:]:
        factor_of = factor_of * one(*cut)
    return factor_of


def bell_draw(rng, extent, spread, most, split=(), kind=jnp.bfloat16):
    result = spread * jax.random.normal(rng, extent, jnp.float32)
    if split:
        result = result * shard_levels(rng, extent, split, -0.22, 0.18)
    return jnp.clip(result, -most, most).astype(kind)


def setup_inputs(seed: int = 0) -> dict:
    seeds = jax.random.split(jax.random.key(seed), 3)
    latent = bell_draw(seeds[0], (3, NX, NY, NZ), 1.0, 6.0, ((1, 8), (2, 8), (3, 4)), jnp.float32)
    cotangent = bell_draw(seeds[1], (3, NX, NY, NZ), 1.0, 6.0, ((1, 8), (2, 8), (3, 4)), jnp.float32)
    return {"latent": latent, "cotangent": cotangent}


SMAX = 0.45
STEP = 0.5
SHORT = 4.0
COUPLE = 0.5
SPREAD = 0.125
KERNEL = (0.05, 0.25, 0.4, 0.25, 0.05)

def cloud(shift):
    return (0.5 * (0.5 - shift) ** 2, 0.75 - shift * shift, 0.5 * (0.5 + shift) ** 2)

def shifted(array, offsets):
    return jnp.roll(array, offsets, axis=(-3, -2, -1))

def paint(shift):
    weights = [cloud(shift[axis]) for axis in range(3)]
    total = jnp.zeros(shift.shape[1:], shift.dtype)
    for first in range(3):
        for second in range(3):
            for third in range(3):
                term = weights[0][first] * weights[1][second] * weights[2][third]
                total = total + shifted(term, (first - 1, second - 1, third - 1))
    return (total, weights)

def read(weights, field):
    total = 0.0
    for first in range(3):
        for second in range(3):
            for third in range(3):
                term = weights[0][first] * weights[1][second] * weights[2][third]
                total = total + term * shifted(field, (1 - first, 1 - second, 1 - third))
    return total

def smooth(field):
    for axis in range(3):
        total = 0.0
        for place in range(5):
            total = total + KERNEL[place] * jnp.roll(field, 2 - place, axis=axis)
        field = total
    return field

def modes(totals):
    squares = 0.0
    kappas = []
    zero = None
    for axis in range(3):
        index = jnp.arange(totals[axis], dtype=jnp.int32)
        angle = index.astype(jnp.float32) * (math.pi / totals[axis])
        shape = [1, 1, 1]
        shape[axis] = totals[axis]
        angle = angle.reshape(shape)
        flag = (index == 0).reshape(shape)
        squares = squares + 4.0 * jnp.sin(angle) ** 2
        kappas.append(jnp.sin(2.0 * angle))
        zero = flag if zero is None else jnp.logical_and(zero, flag)
    gain = jnp.where(zero, 0.0, COUPLE * jnp.exp(-SPREAD * squares) / jnp.where(zero, 1.0, squares))
    return (kappas, gain)

def coarse_force(density):
    sizes = (NX // FACTOR, NY // FACTOR, NZ // FACTOR)
    coarse = density.reshape(sizes[0], FACTOR, sizes[1], FACTOR, sizes[2], FACTOR).sum(axis=(1, 3, 5))
    spectrum = jnp.fft.fftn(coarse)
    kappas, gain = modes(sizes)
    return jnp.stack([jnp.real(jnp.fft.ifftn(1j * (kappa * gain) * spectrum)) for kappa in kappas])

def upsample(coarse):
    for axis in (1, 2, 3):
        coarse = jnp.repeat(coarse, FACTOR, axis=axis)
    return coarse

def advance(latent):
    shift = SMAX * jnp.tanh(latent)
    density, weights = paint(shift)
    potential = -SHORT * smooth(density)
    near = jnp.stack([-(jnp.roll(potential, -1, axis) - jnp.roll(potential, 1, axis)) * 0.5 for axis in range(3)])
    far = upsample(coarse_force(density))
    return shift + STEP * (read(weights, near) + far)

def reference(latent, cotangent):
    moved, pullback = jax.vjp(advance, latent)
    grad_latent = pullback(cotangent)[0]
    return (moved, grad_latent)
```

```python
import functools
import math

import jax
import jax.numpy as jnp
import numpy as np
from jax import lax
from jax.experimental import pallas as pl
from jax.experimental.pallas import tpu as pltpu
from jax.sharding import PartitionSpec as P

SMAX = 0.45
STEP = 0.5
SHORT = 4.0
COUPLE = 0.5
SPREAD = 0.125
KERNEL = (0.05, 0.25, 0.4, 0.25, 0.05)
MESH = pl.DeviceIdType.MESH

BX, BY, BZ = 8, 16, 128
CX, CY, CZ = 4, 8, 64
WX, WY = 16, 24


def basis(length):
    n = np.arange(length)
    angle = 2.0 * np.pi * ((n[:, None] * n[None, :]) % length) / length
    return (np.cos(angle) + np.sin(angle)) / math.sqrt(length)


def five(delta):
    return np.where(np.abs(delta) <= 2, np.take(np.array(KERNEL), np.clip(delta + 2, 0, 4)), 0.0)


def same(left, right):
    return (left[:, None] == right[None, :]).astype(np.float64)


def central(left, right):
    return 0.5 * (same(left + 1, right) - same(left - 1, right))


def make_tables(ngx, ngy, ngz):
    mx, my, mz = CX * ngy, CY * ngz, CZ * ngx
    qx, qy, qz = basis(mx), basis(my), basis(mz)
    f = {}
    cxe, cye = np.arange(-1, CX + 1), np.arange(-1, CY + 1)
    fx, fy = np.arange(-1, BX + 1), np.arange(-4, BY + 4)
    ox, oy, oz = np.arange(BX), np.arange(BY), np.arange(BZ)
    down = lambda v: np.floor_divide(v, 2)

    def rows64(matrix):
        return np.concatenate([matrix, np.zeros((64 - matrix.shape[0], matrix.shape[1]))])

    f["cd"] = rows64(np.kron(same(cxe, down(fx)), same(cye, down(fy)) * ((fy >= -1) & (fy <= BY))))
    own_x, own_y = same(cxe, down(ox)), same(cye, down(oy))
    f["cp"] = rows64(
        np.concatenate(
            [
                np.kron(-central(cxe, down(ox)), own_y),
                np.kron(own_x, -central(cye, down(oy))),
                np.kron(own_x, own_y),
            ],
            axis=1,
        )
    )
    zt = np.zeros((ngx, 512, ngx, 2, CZ))
    for c in range(ngx):
        zc = CZ * c + down(oz)
        q = qz.reshape(mz, ngx, CZ)
        zt[c, 0:128, :, 0] = q[zc % mz]
        zt[c, 128, :, 0] = q[(CZ * c + CZ) % mz]
        zt[c, 255, :, 0] = q[(CZ * c - 1) % mz]
        zt[c, 256:384, :, 1] = q[zc % mz]
        zt[c, 384:512, :, 1] = 0.5 * (q[(zc + 1) % mz] - q[(zc - 1) % mz])
    f["zt"] = zt.reshape(ngx, 512, ngx * 128)
    yt = np.zeros((ngz, ngz, 6, CY, 64))
    for b in range(ngz):
        for x in range(6):
            for y in range(10):
                yt[b, :, x, :, x * 10 + y] = qy[(CY * b + y - 1) % my].reshape(ngz, CY)
    f["yt"] = yt.reshape(ngz, ngz * 48, 64)
    xf = np.zeros((mx, CY, ngy, 6, CY))
    xi = np.zeros((ngy, 6, CY, mx, CY))
    for a in range(ngy):
        for x in range(6):
            for m in range(CY):
                xf[:, m, a, x, m] = qx[(CX * a + x - 1) % mx]
                xi[a, x, m, :, m] = qx[(CX * a + x - 1) % mx]
    f["xf"] = xf.reshape(mx * CY, ngy * 48)
    f["xi"] = xi.reshape(ngy, 48, mx * CY)
    square = lambda total: 4.0 * np.sin(np.pi * np.arange(total) / total) ** 2
    ka = square(mx)[None, :, None] + square(my).reshape(ngz, 1, CY)
    f["ka"] = np.broadcast_to(ka.reshape(ngz, mx * CY, 1), (ngz, mx * CY, 128))
    kb = np.concatenate([square(mz).reshape(ngx, CZ)] * 2, axis=1)
    f["kb"] = np.broadcast_to(kb[:, None], (ngx, 8, 128))
    yi = np.zeros((ngz, 64, ngz, 6, CY))
    for b in range(ngz):
        for x in range(6):
            for y in range(10):
                yi[b, x * 10 + y, :, x, :] = qy[(CY * b + y - 1) % my].reshape(ngz, CY)
    f["yi"] = yi.reshape(ngz, 64, ngz * 48)
    zi = np.zeros((ngx, ngx, 2, CZ, 640))
    for c in range(ngx):
        at = lambda cell: qz[(CZ * c + cell) % mz].T.reshape(ngx, CZ, 128)
        zi[c, :, 0, :, 0:128] = at(down(oz))
        zi[c, :, 0, :, 128:256] = 0.5 * (at(down(oz) + 1) - at(down(oz) - 1))
        for k in range(3):
            zi[c, :, 1, :, 256 + 128 * k : 384 + 128 * k] = at(down(oz + k - 1))
    f["zi"] = zi.reshape(ngx, ngx * 128, 640)
    pad4 = lambda matrix: np.concatenate([matrix, np.zeros((matrix.shape[0], 4))], axis=1)
    f["uf"] = np.stack(
        [
            pad4(np.kron(central(down(ox), cxe), same(down(oy), cye))),
            pad4(np.kron(same(down(ox), cxe), central(down(oy), cye))),
            pad4(np.kron(same(down(ox), cxe), same(down(oy), cye))),
        ]
    )
    ry = np.arange(-1, WY - 1)
    row = ((ry <= BY) * 1.0)[:, None]
    f["up"] = pad4(np.kron(same(down(fx), cxe), same(down(ry), cye) * row))
    zw = np.concatenate([oz, oz + 128])
    zw[252:256] = np.arange(-4, 0)
    valid = np.concatenate([np.ones(128), np.ones(4), np.zeros(120), np.ones(4)])[:, None]
    tap = lambda target, extra: five(target[None, :] + extra - zw[:, None]) * valid
    f["sz"] = np.concatenate(
        [tap(oz + k, 0) for k in (-1, 0, 1)]
        + [tap(oz + k, 1) - tap(oz + k, -1) for k in (-1, 0, 1)],
        axis=1,
    )
    wx, wy = np.arange(-4, WX - 4), np.arange(-4, WY - 4)
    kx = lambda extra: five(fx[:, None] + extra - wx[None, :])
    ky = lambda extra: five(ry[:, None] + extra - wy[None, :]) * row
    half = 0.5 * SHORT
    f["an"] = np.stack(
        [
            half * np.kron(kx(1) - kx(-1), ky(0)),
            half * np.kron(kx(0), ky(1) - ky(-1)),
            half * np.kron(kx(0), ky(0)),
        ]
    )
    return {name: np.ascontiguousarray(value, dtype=np.float32) for name, value in f.items()}


def dot(left, right):
    return jnp.dot(
        left, right, precision=lax.Precision.HIGHEST, preferred_element_type=jnp.float32
    )


NAMES = ("cd", "cp", "zt", "yt", "xf", "xi", "ka", "kb", "yi", "zi", "uf", "up", "sz", "an")
AXIS_OF = {"zt": "gx", "yt": "gz", "xi": "gy", "ka": "gz", "kb": "gx", "yi": "gz", "zi": "gx"}


def kernel(sizes, lat, cot, *refs):
    ngx, ngy, ngz = sizes
    tables = dict(zip(NAMES, refs[: len(NAMES)]))
    moved, grad = refs[len(NAMES) : len(NAMES) + 2]
    rest = refs[len(NAMES) + 2 :]
    local = dict(zip(NAMES, rest[: len(NAMES)]))
    (
        bent, wt, vals, bk, f0, t1, hp, tsend, trecv, yrecv, yhrecv, xrecv, xhrecv,
        zbuf, zrecv, ybuf, yrec, xrec, urec, wrec, near, psi, part,
        table_sem, s_z, r_z, s_y, r_y, s_u, r_u, s_w, r_w, s_x, r_x, s_h, r_h,
    ) = rest[len(NAMES) :]
    c, a, b = lax.axis_index("gx"), lax.axis_index("gy"), lax.axis_index("gz")
    place = {"gx": c, "gy": a, "gz": b}
    size = {"gx": ngx, "gy": ngy, "gz": ngz}

    loads = {}
    for number, name in enumerate(NAMES):
        source = tables[name]
        if name in AXIS_OF:
            source = source.at[place[AXIS_OF[name]]]
        loads[name] = pltpu.make_async_copy(source, local[name], table_sem.at[number])
        loads[name].start()

    def other(axis, step):
        return {axis: lax.rem(place[axis] + step, size[axis])}

    barrier = pltpu.get_barrier_semaphore()
    partners = [(axis, step) for axis in size for step in range(1, size[axis])]
    for axis, step in partners:
        pl.semaphore_signal(barrier, inc=1, device_id=other(axis, step), device_id_type=MESH)

    started = []

    def send(source, target, send_sem, recv_sem, axis, step):
        copy = pltpu.make_async_remote_copy(
            src_ref=source,
            dst_ref=target,
            send_sem=send_sem,
            recv_sem=recv_sem,
            device_id=other(axis, step),
            device_id_type=MESH,
        )
        copy.start()
        return copy

    lane = lax.broadcasted_iota(jnp.int32, (WY, 128), 1)
    edge = jnp.logical_or(lane < 4, lane >= 124)
    upper = lax.rem(lane, 8) >= 4

    wt[...] = jnp.zeros_like(wt)
    f0[...] = jnp.zeros_like(f0)
    t1[...] = jnp.zeros_like(t1)
    hp[...] = jnp.zeros_like(hp)
    vals[...] = jnp.zeros_like(vals)
    bk[...] = jnp.zeros_like(bk)
    for axis in range(3):
        bend = jnp.tanh(lat[axis])
        bent[axis] = bend
        shift = SMAX * bend
        wt[3 * axis, 2:10, 8:24] = 0.5 * (0.5 - shift) ** 2
        wt[3 * axis + 1, 2:10, 8:24] = 0.75 - shift * shift
        wt[3 * axis + 2, 2:10, 8:24] = 0.5 * (0.5 + shift) ** 2
        vals[axis, 2:10, 8:24] = STEP * cot[axis]

    def gathered(plane, charges):
        totals = [[None] * 3 for _ in range(charges or 1)]
        for i in range(3):
            at = plane + 2 - i
            for j in range(3):
                rows = pl.ds(5 - j, WY)
                cross = wt[i, at, rows, :] * wt[3 + j, at, rows, :]
                for k in range(3):
                    weight = cross * wt[6 + k, at, rows, :]
                    for q in range(charges or 1):
                        term = weight * vals[q, at, rows, :] if charges else weight
                        totals[q][k] = term if totals[q][k] is None else totals[q][k] + term
        return totals

    def paint(plane, carry):
        ((low, middle, high),) = gathered(plane, 0)
        low = pltpu.roll(low, 127, 1)
        high = pltpu.roll(high, 1, 1)
        keep_low, keep_high = lane < 127, lane >= 1
        main = middle + jnp.where(keep_low, low, 0.0) + jnp.where(keep_high, high, 0.0)
        spill = jnp.where(keep_low, 0.0, low) + jnp.where(keep_high, 0.0, high)
        f0[0, plane + 3] = main
        t1[0, plane + 3] = spill
        return carry

    lax.fori_loop(0, BX + 2, paint, 0)

    loads["cd"].wait()
    loads["cp"].wait()
    inner = BX + 2
    density = jnp.concatenate(
        [f0[0, 3:13].reshape(inner * WY, 128), t1[0, 3:13].reshape(inner * WY, 128)], axis=1
    )
    rho = dot(local["cd"][...], density)
    pushed = [(STEP * cot[axis]).reshape(BX * BY, 128) for axis in range(3)]
    cross_source = dot(local["cp"][:, 0:256], jnp.concatenate(pushed[:2], axis=0))
    along_source = dot(local["cp"][:, 256:384], pushed[2])
    loads["zt"].wait()
    modes = dot(jnp.concatenate([rho, cross_source, along_source], axis=1), local["zt"][...])
    for j in range(ngx):
        zbuf[j] = modes[:, 128 * j : 128 * (j + 1)]
    pl.semaphore_wait(barrier, len(partners))
    z_copies = [
        send(zbuf.at[lax.rem(c + d, ngx)], zrecv.at[d], s_z.at[d], r_z.at[d], "gx", d)
        for d in range(1, ngx)
    ]
    started += z_copies

    def paint_back(plane, carry):
        totals = gathered(plane, 3)
        for q in range(3):
            for k in range(3):
                bk[3 * q + k, plane + 2, 8:32, :] = totals[q][k]
        return carry

    lax.fori_loop(0, BX + 2, paint_back, 0)

    def spread_back(plane, carry):
        at = plane + 1

        def cross(k):
            return 0.5 * (
                bk[k, at + 1, 8:32, :] - bk[k, at - 1, 8:32, :]
                + bk[3 + k, at, 9:33, :] - bk[3 + k, at, 7:31, :]
            )

        up = [0.5 * bk[6 + k, at, 8:32, :] for k in range(3)]
        parts = {
            -2: up[0],
            -1: cross(0) + up[1],
            1: cross(2) - up[1],
            2: -up[2],
        }
        main = cross(1) + up[2] - up[0]
        spill = None
        for step, value in parts.items():
            rolled = pltpu.roll(value, step % 128, 1)
            keep = lane >= step if step > 0 else lane < 128 + step
            main = main + jnp.where(keep, rolled, 0.0)
            over = jnp.where(keep, 0.0, rolled)
            spill = over if spill is None else spill + over
        f0[1, plane + 2] = main
        t1[1, plane + 2] = spill
        return carry

    lax.fori_loop(0, BX + 4, spread_back, 0)

    def pack(plane, carry):
        by = 8 * plane + 4
        out = []
        for q in range(2):
            out.append(carry[2 * q] + pltpu.roll(jnp.where(edge, f0[q, plane], 0.0), by, 1))
            out.append(carry[2 * q + 1] + pltpu.roll(t1[q, plane], by, 1))
        return tuple(out)

    empty = jnp.zeros((WY, 128), jnp.float32)
    packed = lax.fori_loop(2, BX + 6, pack, (empty,) * 4)
    for q in range(2):
        face, spill = packed[2 * q], packed[2 * q + 1]
        tsend[0, q] = jnp.where(upper, spill, face)
        tsend[1, q] = jnp.where(upper, face, spill)
        hp[q] = spill
    t_copies = [
        send(tsend.at[0], trecv.at[0], s_h.at[0], r_h.at[0], "gx", 1),
        send(tsend.at[1], trecv.at[1], s_h.at[1], r_h.at[1], "gx", ngx - 1),
    ]
    started += t_copies

    for copy in z_copies:
        copy.wait_recv()
    total = zbuf[c]
    for d in range(1, ngx):
        total = total + zrecv[d]
    loads["yt"].wait()
    ybuf[...] = dot(local["yt"][...], total).reshape(ngz, 48, 128)
    y_copies = [
        send(ybuf.at[lax.rem(b + d, ngz)], yrec.at[d], s_y.at[d], r_y.at[d], "gz", d)
        for d in range(1, ngz)
    ]
    started += y_copies

    for copy in t_copies:
        copy.wait_recv()
    fixes = []
    for q in range(2):
        from_left, from_right = trecv[0, q], trecv[1, q]
        hp[q] = hp[q] + jnp.where(upper, from_right, from_left)
        fixes.append(jnp.where(upper, from_left, from_right))

    def fix(plane, carry):
        by = 124 - 8 * plane
        by = jnp.where(by < 0, by + 128, by)
        for q in range(2):
            f0[q, plane] = f0[q, plane] + jnp.where(edge, pltpu.roll(fixes[q], by, 1), 0.0)
        return carry

    lax.fori_loop(2, BX + 6, fix, 0)
    rim_copies = [
        send(f0.at[:, 2:14, 16:24], yrecv.at[0], s_h.at[2], r_h.at[2], "gz", 1),
        send(f0.at[:, 2:14, 0:8], yrecv.at[1], s_h.at[3], r_h.at[3], "gz", ngz - 1),
        send(hp.at[:, 16:24], yhrecv.at[0], s_h.at[4], r_h.at[4], "gz", 1),
        send(hp.at[:, 0:8], yhrecv.at[1], s_h.at[5], r_h.at[5], "gz", ngz - 1),
    ]

    for copy in y_copies:
        copy.wait_recv()
    total = ybuf[b]
    for d in range(1, ngz):
        total = total + yrec[d]
    xrec[a] = total
    x_copies = [
        send(xrec.at[a], xrec.at[a], s_x.at[d], r_x.at[d], "gy", d) for d in range(1, ngy)
    ]
    started += x_copies

    for copy in rim_copies:
        copy.wait()
    f0[:, 2:14, 0:8] = f0[:, 2:14, 0:8] + yrecv[0]
    f0[:, 2:14, 16:24] = f0[:, 2:14, 16:24] + yrecv[1]
    hp[:, 0:8] = hp[:, 0:8] + yhrecv[0]
    hp[:, 16:24] = hp[:, 16:24] + yhrecv[1]
    side_copies = [
        send(f0.at[0, 8:13], xrecv.at[0, 0], s_h.at[6], r_h.at[6], "gy", 1),
        send(f0.at[1, 9:14], xrecv.at[0, 1], s_h.at[7], r_h.at[7], "gy", 1),
        send(f0.at[0, 3:8], xrecv.at[1, 0], s_h.at[8], r_h.at[8], "gy", ngy - 1),
        send(f0.at[1, 2:7], xrecv.at[1, 1], s_h.at[9], r_h.at[9], "gy", ngy - 1),
        send(hp, xhrecv.at[0], s_h.at[10], r_h.at[10], "gy", 1),
        send(hp, xhrecv.at[1], s_h.at[11], r_h.at[11], "gy", ngy - 1),
    ]

    loads["ka"].wait()
    loads["kb"].wait()
    squares = local["ka"][...] + local["kb"][0:1, :]
    zero = squares == 0.0
    gain = jnp.where(
        zero, 0.0, COUPLE * jnp.exp(-SPREAD * squares) / jnp.where(zero, 1.0, squares)
    )
    loads["xf"].wait()
    loads["xi"].wait()
    for copy in x_copies:
        copy.wait_recv()
    spectrum = dot(local["xf"][...], xrec[...].reshape(ngy * 48, 128))
    urec[b] = dot(local["xi"][...], gain * spectrum)
    u_copies = [
        send(urec.at[b], urec.at[b], s_u.at[d], r_u.at[d], "gz", d) for d in range(1, ngz)
    ]
    started += u_copies

    for copy in side_copies:
        copy.wait()
    f0[0, 0:5] = f0[0, 0:5] + xrecv[0, 0]
    f0[1, 1:6] = f0[1, 1:6] + xrecv[0, 1]
    f0[0, 11:16] = f0[0, 11:16] + xrecv[1, 0]
    f0[1, 10:15] = f0[1, 10:15] + xrecv[1, 1]
    rims = [
        hp[q]
        + jnp.where(
            lane < 64, pltpu.roll(xhrecv[0, q], 64, 1), pltpu.roll(xhrecv[1, q], 64, 1)
        )
        for q in range(2)
    ]

    def unpack(plane, carry):
        by = 124 - 8 * plane
        by = jnp.where(by < 0, by + 128, by)
        for q in range(2):
            t1[q, plane] = jnp.where(edge, pltpu.roll(rims[q], by, 1), 0.0)
        return carry

    lax.fori_loop(0, WX, unpack, 0)
    window = [
        jnp.concatenate([f0[q].reshape(WX * WY, 128), t1[q].reshape(WX * WY, 128)], axis=1)
        for q in range(2)
    ]
    loads["sz"].wait()
    loads["an"].wait()

    def keep(target, slot, value):
        for k in range(3):
            target[slot, k] = value[:, 128 * k : 128 * (k + 1)].reshape(inner, WY, 128)

    smoothed = dot(window[0], local["sz"][:, 0:384])
    keep(near, 0, dot(local["an"][0], smoothed))
    keep(near, 1, dot(local["an"][1], smoothed))
    keep(near, 2, dot(local["an"][2], dot(window[0], local["sz"][:, 384:768])))
    keep(near, 3, -2.0 * dot(local["an"][2], dot(window[1], local["sz"][:, 0:384])))

    loads["yi"].wait()
    for copy in u_copies:
        copy.wait_recv()
    wrec[c] = dot(local["yi"][...], urec[...].reshape(ngz * 48, 128))
    w_copies = [
        send(wrec.at[c], wrec.at[c], s_w.at[d], r_w.at[d], "gx", d) for d in range(1, ngx)
    ]
    started += w_copies

    def slopes(plane):
        rows = pl.ds(8, BY)
        weights = [wt[n, plane + 2, rows, :] for n in range(9)]
        slope = []
        for axis in range(3):
            shift = SMAX * bent[axis, plane]
            slope += [shift - 0.5, -2.0 * shift, shift + 0.5]
        return weights, slope

    def plus(total, term):
        return term if total is None else total + term

    def read(plane, carry):
        weights, slope = slopes(plane)
        pushes = [vals[axis, plane + 2, 8:24, :] for axis in range(3)]
        sums = [None] * 6
        for k in range(3):
            mid = [None] * 6
            for j in range(3):
                line = [None] * 5
                for i in range(3):
                    at = [near[q, k, plane + i, pl.ds(j, BY), :] for q in range(4)]
                    both = at[3]
                    for q in range(3):
                        line[q] = plus(line[q], weights[i] * at[q])
                        both = both + pushes[q] * at[q]
                    line[3] = plus(line[3], weights[i] * both)
                    line[4] = plus(line[4], slope[i] * both)
                for q in range(3):
                    mid[q] = plus(mid[q], weights[3 + j] * line[q])
                mid[3] = plus(mid[3], weights[3 + j] * line[4])
                mid[4] = plus(mid[4], slope[3 + j] * line[3])
                mid[5] = plus(mid[5], weights[3 + j] * line[3])
            for q in range(5):
                sums[q] = plus(sums[q], weights[6 + k] * mid[q])
            sums[5] = plus(sums[5], slope[6 + k] * mid[5])
        for q in range(6):
            part[q, plane] = sums[q]
        return carry

    lax.fori_loop(0, BX, read, 0)

    for name in ("zi", "uf", "up"):
        loads[name].wait()
    for copy in w_copies:
        copy.wait_recv()
    spread = dot(jnp.concatenate([wrec[d] for d in range(ngx)], axis=1), local["zi"][...])
    value, slant = spread[:, 0:128], spread[:, 128:256]
    far = [
        dot(local["uf"][0], value),
        dot(local["uf"][1], value),
        dot(local["uf"][2], slant),
    ]
    fine = dot(local["up"][...], spread[:, 256:640])
    for k in range(3):
        psi[k] = fine[:, 128 * k : 128 * (k + 1)].reshape(inner, WY, 128)
    for axis in range(3):
        moved[axis] = SMAX * bent[axis] + STEP * (
            part[axis] + far[axis].reshape(BX, BY, 128)
        )

    def finish(plane, carry):
        weights, slope = slopes(plane)
        sums = [part[3 + axis, plane] for axis in range(3)]
        for k in range(3):
            mid = [None] * 3
            for j in range(3):
                line = [None] * 2
                for i in range(3):
                    at = psi[k, plane + i, pl.ds(j, BY), :]
                    line[0] = plus(line[0], weights[i] * at)
                    line[1] = plus(line[1], slope[i] * at)
                mid[0] = plus(mid[0], weights[3 + j] * line[1])
                mid[1] = plus(mid[1], slope[3 + j] * line[0])
                mid[2] = plus(mid[2], weights[3 + j] * line[0])
            sums[0] = sums[0] + weights[6 + k] * mid[0]
            sums[1] = sums[1] + weights[6 + k] * mid[1]
            sums[2] = sums[2] + slope[6 + k] * mid[2]
        for axis in range(3):
            bend = bent[axis, plane]
            grad[axis, plane] = (cot[axis, plane] + sums[axis]) * (SMAX * (1.0 - bend * bend))
        return carry

    lax.fori_loop(0, BX, finish, 0)
    for copy in started:
        copy.wait_send()


def body(tables, sizes, latent, cotangent):
    ngx, ngy, ngz = sizes
    dma = pltpu.SemaphoreType.DMA
    f32 = jnp.float32

    def vmem(*shape):
        return pltpu.VMEM(shape, f32)

    arrays = [jnp.asarray(tables[name]) for name in NAMES]
    locals_ = [
        vmem(*(array.shape[1:] if name in AXIS_OF else array.shape))
        for name, array in zip(NAMES, arrays)
    ]
    scratch = [
        vmem(3, BX, BY, 128),
        vmem(9, 12, 32, 128),
        vmem(3, 12, 32, 128),
        vmem(9, 14, 40, 128),
        vmem(2, WX, WY, 128),
        vmem(2, WX, WY, 128),
        vmem(2, WY, 128),
        vmem(2, 2, WY, 128),
        vmem(2, 2, WY, 128),
        vmem(2, 2, 12, 8, 128),
        vmem(2, 2, 8, 128),
        vmem(2, 2, 5, WY, 128),
        vmem(2, 2, WY, 128),
        vmem(ngx, 64, 128),
        vmem(ngx, 64, 128),
        vmem(ngz, 48, 128),
        vmem(ngz, 48, 128),
        vmem(ngy, 48, 128),
        vmem(ngz, 48, 128),
        vmem(ngx, 64, 128),
        vmem(4, 3, BX + 2, WY, 128),
        vmem(3, BX + 2, WY, 128),
        vmem(6, BX, BY, 128),
        dma((len(NAMES),)),
        dma((ngx,)), dma((ngx,)),
        dma((ngz,)), dma((ngz,)),
        dma((ngz,)), dma((ngz,)),
        dma((ngx,)), dma((ngx,)),
        dma((ngy,)), dma((ngy,)),
        dma((12,)), dma((12,)),
    ]
    whole = pl.BlockSpec(memory_space=pltpu.VMEM)
    return pl.pallas_call(
        functools.partial(kernel, sizes),
        out_shape=[jax.ShapeDtypeStruct((3, BX, BY, BZ), f32)] * 2,
        in_specs=[whole, whole] + [pl.BlockSpec(memory_space=pl.ANY)] * len(NAMES),
        out_specs=[whole, whole],
        scratch_shapes=locals_ + scratch,
        compiler_params=pltpu.CompilerParams(
            collective_id=0, has_side_effects=True, vmem_limit_bytes=48 * 1024 * 1024
        ),
    )(latent, cotangent, *arrays)


def solution(mesh):
    sizes = (mesh.shape["gx"], mesh.shape["gy"], mesh.shape["gz"])
    tables = make_tables(*sizes)
    placed = P(None, "gy", "gz", "gx")
    return jax.shard_map(
        functools.partial(body, tables, sizes),
        mesh=mesh,
        in_specs=(placed, placed),
        out_specs=(placed, placed),
        check_vma=False,
    )
```

```python
import functools
import math

import jax
import jax.numpy as jnp
import ml_dtypes
import numpy as np
from jax import lax
from jax.experimental import pallas as pl
from jax.experimental.pallas import tpu as pltpu
from jax.sharding import PartitionSpec as P

SMAX = 0.45
STEP = 0.5
SHORT = 4.0
COUPLE = 0.5
SPREAD = 0.125
KERNEL = (0.05, 0.25, 0.4, 0.25, 0.05)
MESH = pl.DeviceIdType.MESH

BX, BY, BZ = 8, 16, 128
CX, CY, CZ = 4, 8, 64
WX, WY = 16, 24


def basis(length):
    n = np.arange(length)
    angle = 2.0 * np.pi * ((n[:, None] * n[None, :]) % length) / length
    return (np.cos(angle) + np.sin(angle)) / math.sqrt(length)


def five(delta):
    return np.where(np.abs(delta) <= 2, np.take(np.array(KERNEL), np.clip(delta + 2, 0, 4)), 0.0)


def same(left, right):
    return (left[:, None] == right[None, :]).astype(np.float64)


def central(left, right):
    return 0.5 * (same(left + 1, right) - same(left - 1, right))


def make_tables(ngx, ngy, ngz):
    mx, my, mz = CX * ngy, CY * ngz, CZ * ngx
    qx, qy, qz = basis(mx), basis(my), basis(mz)
    f = {}
    cxe, cye = np.arange(-1, CX + 1), np.arange(-1, CY + 1)
    fx, fy = np.arange(-1, BX + 1), np.arange(-4, BY + 4)
    ox, oy, oz = np.arange(BX), np.arange(BY), np.arange(BZ)
    down = lambda v: np.floor_divide(v, 2)

    def rows64(matrix):
        return np.concatenate([matrix, np.zeros((64 - matrix.shape[0], matrix.shape[1]))])

    f["cd"] = rows64(np.kron(same(cxe, down(fx)), same(cye, down(fy)) * ((fy >= -1) & (fy <= BY))))
    own_x, own_y = same(cxe, down(ox)), same(cye, down(oy))
    f["cp"] = rows64(
        np.concatenate(
            [
                np.kron(-central(cxe, down(ox)), own_y),
                np.kron(own_x, -central(cye, down(oy))),
                np.kron(own_x, own_y),
            ],
            axis=1,
        )
    )
    zt = np.zeros((ngx, 512, ngx, 2, CZ))
    for c in range(ngx):
        zc = CZ * c + down(oz)
        q = qz.reshape(mz, ngx, CZ)
        zt[c, 0:128, :, 0] = q[zc % mz]
        zt[c, 128, :, 0] = q[(CZ * c + CZ) % mz]
        zt[c, 255, :, 0] = q[(CZ * c - 1) % mz]
        zt[c, 256:384, :, 1] = q[zc % mz]
        zt[c, 384:512, :, 1] = 0.5 * (q[(zc + 1) % mz] - q[(zc - 1) % mz])
    f["zt"] = zt.reshape(ngx, 512, ngx * 128)
    yt = np.zeros((ngz, ngz, 6, CY, 64))
    for b in range(ngz):
        for x in range(6):
            for y in range(10):
                yt[b, :, x, :, x * 10 + y] = qy[(CY * b + y - 1) % my].reshape(ngz, CY)
    f["yt"] = yt.reshape(ngz, ngz * 48, 64)
    xf = np.zeros((mx, CY, ngy, 6, CY))
    xi = np.zeros((ngy, 6, CY, mx, CY))
    for a in range(ngy):
        for x in range(6):
            for m in range(CY):
                xf[:, m, a, x, m] = qx[(CX * a + x - 1) % mx]
                xi[a, x, m, :, m] = qx[(CX * a + x - 1) % mx]
    f["xf"] = xf.reshape(mx * CY, ngy * 48)
    f["xi"] = xi.reshape(ngy, 48, mx * CY)
    square = lambda total: 4.0 * np.sin(np.pi * np.arange(total) / total) ** 2
    ka = square(mx)[None, :, None] + square(my).reshape(ngz, 1, CY)
    f["ka"] = np.broadcast_to(ka.reshape(ngz, mx * CY, 1), (ngz, mx * CY, 128))
    kb = np.concatenate([square(mz).reshape(ngx, CZ)] * 2, axis=1)
    f["kb"] = np.broadcast_to(kb[:, None], (ngx, 8, 128))
    yi = np.zeros((ngz, 64, ngz, 6, CY))
    for b in range(ngz):
        for x in range(6):
            for y in range(10):
                yi[b, x * 10 + y, :, x, :] = qy[(CY * b + y - 1) % my].reshape(ngz, CY)
    f["yi"] = yi.reshape(ngz, 64, ngz * 48)
    zi = np.zeros((ngx, ngx, 2, CZ, 640))
    for c in range(ngx):
        at = lambda cell: qz[(CZ * c + cell) % mz].T.reshape(ngx, CZ, 128)
        zi[c, :, 0, :, 0:128] = at(down(oz))
        zi[c, :, 0, :, 128:256] = 0.5 * (at(down(oz) + 1) - at(down(oz) - 1))
        for k in range(3):
            zi[c, :, 1, :, 256 + 128 * k : 384 + 128 * k] = at(down(oz + k - 1))
    f["zi"] = zi.reshape(ngx, ngx * 128, 640)
    pad4 = lambda matrix: np.concatenate([matrix, np.zeros((matrix.shape[0], 4))], axis=1)
    f["uf"] = np.stack(
        [
            pad4(np.kron(central(down(ox), cxe), same(down(oy), cye))),
            pad4(np.kron(same(down(ox), cxe), central(down(oy), cye))),
            pad4(np.kron(same(down(ox), cxe), same(down(oy), cye))),
        ]
    )
    ry = np.arange(-1, WY - 1)
    row = ((ry <= BY) * 1.0)[:, None]
    f["up"] = pad4(np.kron(same(down(fx), cxe), same(down(ry), cye) * row))
    zw = np.concatenate([oz, oz + 128])
    zw[252:256] = np.arange(-4, 0)
    valid = np.concatenate([np.ones(128), np.ones(4), np.zeros(120), np.ones(4)])[:, None]
    tap = lambda target, extra: five(target[None, :] + extra - zw[:, None]) * valid
    f["sz"] = np.concatenate(
        [tap(oz + k, 0) for k in (-1, 0, 1)]
        + [tap(oz + k, 1) - tap(oz + k, -1) for k in (-1, 0, 1)],
        axis=1,
    )
    wx, wy = np.arange(-4, WX - 4), np.arange(-4, WY - 4)
    kx = lambda extra: five(fx[:, None] + extra - wx[None, :])
    ky = lambda extra: five(ry[:, None] + extra - wy[None, :]) * row
    half = 0.5 * SHORT
    f["an"] = np.stack(
        [
            half * np.kron(kx(1) - kx(-1), ky(0)),
            half * np.kron(kx(0), ky(1) - ky(-1)),
            half * np.kron(kx(0), ky(0)),
        ]
    )
    f["cq"], f["c0"] = f["cp"][:, 0:256], f.pop("cp")[:, 256:384]
    tables = {}
    for name, value in f.items():
        if name not in AXIS_OF:
            value = value[None]
        value = value.astype(np.float32)
        if name in LEFT or name in RIGHT:
            high = value.astype(ml_dtypes.bfloat16)
            low = (value - high.astype(np.float32)).astype(ml_dtypes.bfloat16)
            value = np.concatenate([high, high, low], axis=-1 if name in LEFT else -2)
        least = -(-TABLE_BYTES // value[0].nbytes)
        filler = np.zeros((max(0, least - len(value)),) + value.shape[1:], value.dtype)
        tables[name] = np.ascontiguousarray(np.concatenate([value, filler]))
    return tables


TABLE_BYTES = 2**21
NAMES = (
    "cd", "cq", "c0", "zt", "yt", "xf", "xi", "ka", "kb", "yi", "sz", "an", "zi", "uf", "up",
)
LEFT = ("cd", "cq", "c0", "yt", "xf", "xi", "yi", "uf", "up", "an")
RIGHT = ("zt", "zi", "sz")


def halves(value):
    high = value.astype(jnp.bfloat16)
    low = (value - high.astype(jnp.float32)).astype(jnp.bfloat16)
    return high, low


def dot(table, value):
    high, low = halves(value)
    stacked = jnp.concatenate([high, low, high], axis=0)
    return jnp.dot(table, stacked, preferred_element_type=jnp.float32)


def rdot(value, table):
    high, low = halves(value)
    stacked = jnp.concatenate([high, low, high], axis=1)
    return jnp.dot(stacked, table, preferred_element_type=jnp.float32)


AXIS_OF = {"zt": "gx", "yt": "gz", "xi": "gy", "ka": "gz", "kb": "gx", "yi": "gz", "zi": "gx"}


def kernel(sizes, lat, cot, *refs):
    ngx, ngy, ngz = sizes
    tables = dict(zip(NAMES, refs[: len(NAMES)]))
    moved, grad = refs[len(NAMES) : len(NAMES) + 2]
    rest = refs[len(NAMES) + 2 :]
    local = dict(zip(NAMES, rest[: len(NAMES)]))
    (
        bent, wt, vals, bk, f0, t1, hp, tsend, trecv, yrecv, yhrecv, xrecv, xhrecv,
        zbuf, zrecv, ybuf, yrec, xrec, urec, wrec, near, psi, part,
        table_sem, s_z, r_z, s_y, r_y, s_u, r_u, s_w, r_w, s_x, r_x, s_h, r_h,
    ) = rest[len(NAMES) :]
    c, a, b = lax.axis_index("gx"), lax.axis_index("gy"), lax.axis_index("gz")
    place = {"gx": c, "gy": a, "gz": b}
    size = {"gx": ngx, "gy": ngy, "gz": ngz}

    loads = {}
    for number, name in enumerate(NAMES):
        source = tables[name].at[place[AXIS_OF[name]] if name in AXIS_OF else 0]
        loads[name] = pltpu.make_async_copy(source, local[name], table_sem.at[number])
        loads[name].start()

    def other(axis, step):
        return {axis: lax.rem(place[axis] + step, size[axis])}

    barrier = pltpu.get_barrier_semaphore()
    partners = [(axis, step) for axis in size for step in range(1, size[axis])]
    for axis, step in partners:
        pl.semaphore_signal(barrier, inc=1, device_id=other(axis, step), device_id_type=MESH)

    started = []

    def send(source, target, send_sem, recv_sem, axis, step):
        copy = pltpu.make_async_remote_copy(
            src_ref=source,
            dst_ref=target,
            send_sem=send_sem,
            recv_sem=recv_sem,
            device_id=other(axis, step),
            device_id_type=MESH,
        )
        copy.start()
        return copy

    lane = lax.broadcasted_iota(jnp.int32, (WY, 128), 1)
    edge = jnp.logical_or(lane < 4, lane >= 124)
    upper = lax.rem(lane, 8) >= 4

    wt[...] = jnp.zeros_like(wt)
    f0[...] = jnp.zeros_like(f0)
    t1[...] = jnp.zeros_like(t1)
    hp[...] = jnp.zeros_like(hp)
    vals[...] = jnp.zeros_like(vals)
    bk[...] = jnp.zeros_like(bk)
    for axis in range(3):
        bend = jnp.tanh(lat[axis])
        bent[axis] = bend
        shift = SMAX * bend
        wt[3 * axis, 2:10, 8:24] = 0.5 * (0.5 - shift) ** 2
        wt[3 * axis + 1, 2:10, 8:24] = 0.75 - shift * shift
        wt[3 * axis + 2, 2:10, 8:24] = 0.5 * (0.5 + shift) ** 2
        vals[axis, 2:10, 8:24] = STEP * cot[axis]

    def gathered(plane, charges):
        totals = [[None] * 3 for _ in range(charges or 1)]
        for i in range(3):
            at = plane + 2 - i
            for j in range(3):
                rows = pl.ds(5 - j, WY)
                cross = wt[i, at, rows, :] * wt[3 + j, at, rows, :]
                for k in range(3):
                    weight = cross * wt[6 + k, at, rows, :]
                    for q in range(charges or 1):
                        term = weight * vals[q, at, rows, :] if charges else weight
                        totals[q][k] = term if totals[q][k] is None else totals[q][k] + term
        return totals

    def paint(plane, carry):
        ((low, middle, high),) = gathered(plane, 0)
        low = pltpu.roll(low, 127, 1)
        high = pltpu.roll(high, 1, 1)
        keep_low, keep_high = lane < 127, lane >= 1
        main = middle + jnp.where(keep_low, low, 0.0) + jnp.where(keep_high, high, 0.0)
        spill = jnp.where(keep_low, 0.0, low) + jnp.where(keep_high, 0.0, high)
        f0[0, plane + 3] = main
        t1[0, plane + 3] = spill
        return carry

    lax.fori_loop(0, BX + 2, paint, 0)

    loads["cd"].wait()
    loads["cq"].wait()
    loads["c0"].wait()
    inner = BX + 2
    density = jnp.concatenate(
        [f0[0, 3:13].reshape(inner * WY, 128), t1[0, 3:13].reshape(inner * WY, 128)], axis=1
    )
    rho = dot(local["cd"][...], density)
    pushed = [(STEP * cot[axis]).reshape(BX * BY, 128) for axis in range(3)]
    cross_source = dot(local["cq"][...], jnp.concatenate(pushed[:2], axis=0))
    along_source = dot(local["c0"][...], pushed[2])
    loads["zt"].wait()
    modes = rdot(jnp.concatenate([rho, cross_source, along_source], axis=1), local["zt"][...])
    for j in range(ngx):
        zbuf[j] = modes[:, 128 * j : 128 * (j + 1)]
    pl.semaphore_wait(barrier, len(partners))
    z_copies = [
        send(zbuf.at[lax.rem(c + d, ngx)], zrecv.at[d], s_z.at[d], r_z.at[d], "gx", d)
        for d in range(1, ngx)
    ]
    started += z_copies

    def paint_back(plane, carry):
        totals = gathered(plane, 3)
        for q in range(3):
            for k in range(3):
                bk[3 * q + k, plane + 2, 8:32, :] = totals[q][k]
        return carry

    lax.fori_loop(0, BX + 2, paint_back, 0)

    def spread_back(plane, carry):
        at = plane + 1

        def cross(k):
            return 0.5 * (
                bk[k, at + 1, 8:32, :] - bk[k, at - 1, 8:32, :]
                + bk[3 + k, at, 9:33, :] - bk[3 + k, at, 7:31, :]
            )

        up = [0.5 * bk[6 + k, at, 8:32, :] for k in range(3)]
        parts = {
            -2: up[0],
            -1: cross(0) + up[1],
            1: cross(2) - up[1],
            2: -up[2],
        }
        main = cross(1) + up[2] - up[0]
        spill = None
        for step, value in parts.items():
            rolled = pltpu.roll(value, step % 128, 1)
            keep = lane >= step if step > 0 else lane < 128 + step
            main = main + jnp.where(keep, rolled, 0.0)
            over = jnp.where(keep, 0.0, rolled)
            spill = over if spill is None else spill + over
        f0[1, plane + 2] = main
        t1[1, plane + 2] = spill
        return carry

    lax.fori_loop(0, BX + 4, spread_back, 0)

    def pack(plane, carry):
        by = 8 * plane + 4
        out = []
        for q in range(2):
            out.append(carry[2 * q] + pltpu.roll(jnp.where(edge, f0[q, plane], 0.0), by, 1))
            out.append(carry[2 * q + 1] + pltpu.roll(t1[q, plane], by, 1))
        return tuple(out)

    empty = jnp.zeros((WY, 128), jnp.float32)
    packed = lax.fori_loop(2, BX + 6, pack, (empty,) * 4)
    for q in range(2):
        face, spill = packed[2 * q], packed[2 * q + 1]
        tsend[0, q] = jnp.where(upper, spill, face)
        tsend[1, q] = jnp.where(upper, face, spill)
        hp[q] = spill
    t_copies = [
        send(tsend.at[0], trecv.at[0], s_h.at[0], r_h.at[0], "gx", 1),
        send(tsend.at[1], trecv.at[1], s_h.at[1], r_h.at[1], "gx", ngx - 1),
    ]
    started += t_copies

    for copy in z_copies:
        copy.wait_recv()
    total = zbuf[c]
    for d in range(1, ngx):
        total = total + zrecv[d]
    loads["yt"].wait()
    ybuf[...] = dot(local["yt"][...], total).reshape(ngz, 48, 128)
    y_copies = [
        send(ybuf.at[lax.rem(b + d, ngz)], yrec.at[d], s_y.at[d], r_y.at[d], "gz", d)
        for d in range(1, ngz)
    ]
    started += y_copies

    for copy in t_copies:
        copy.wait_recv()
    fixes = []
    for q in range(2):
        from_left, from_right = trecv[0, q], trecv[1, q]
        hp[q] = hp[q] + jnp.where(upper, from_right, from_left)
        fixes.append(jnp.where(upper, from_left, from_right))

    def fix(plane, carry):
        by = 124 - 8 * plane
        by = jnp.where(by < 0, by + 128, by)
        for q in range(2):
            f0[q, plane] = f0[q, plane] + jnp.where(edge, pltpu.roll(fixes[q], by, 1), 0.0)
        return carry

    lax.fori_loop(2, BX + 6, fix, 0)
    rim_copies = [
        send(f0.at[:, 2:14, 16:24], yrecv.at[0], s_h.at[2], r_h.at[2], "gz", 1),
        send(f0.at[:, 2:14, 0:8], yrecv.at[1], s_h.at[3], r_h.at[3], "gz", ngz - 1),
        send(hp.at[:, 16:24], yhrecv.at[0], s_h.at[4], r_h.at[4], "gz", 1),
        send(hp.at[:, 0:8], yhrecv.at[1], s_h.at[5], r_h.at[5], "gz", ngz - 1),
    ]

    for copy in y_copies:
        copy.wait_recv()
    total = ybuf[b]
    for d in range(1, ngz):
        total = total + yrec[d]
    xrec[a] = total
    x_copies = [
        send(xrec.at[a], xrec.at[a], s_x.at[d], r_x.at[d], "gy", d) for d in range(1, ngy)
    ]
    started += x_copies

    for copy in rim_copies:
        copy.wait()
    f0[:, 2:14, 0:8] = f0[:, 2:14, 0:8] + yrecv[0]
    f0[:, 2:14, 16:24] = f0[:, 2:14, 16:24] + yrecv[1]
    hp[:, 0:8] = hp[:, 0:8] + yhrecv[0]
    hp[:, 16:24] = hp[:, 16:24] + yhrecv[1]
    side_copies = [
        send(f0.at[0, 8:13], xrecv.at[0, 0], s_h.at[6], r_h.at[6], "gy", 1),
        send(f0.at[1, 9:14], xrecv.at[0, 1], s_h.at[7], r_h.at[7], "gy", 1),
        send(f0.at[0, 3:8], xrecv.at[1, 0], s_h.at[8], r_h.at[8], "gy", ngy - 1),
        send(f0.at[1, 2:7], xrecv.at[1, 1], s_h.at[9], r_h.at[9], "gy", ngy - 1),
        send(hp, xhrecv.at[0], s_h.at[10], r_h.at[10], "gy", 1),
        send(hp, xhrecv.at[1], s_h.at[11], r_h.at[11], "gy", ngy - 1),
    ]

    loads["ka"].wait()
    loads["kb"].wait()
    squares = local["ka"][...] + local["kb"][0:1, :]
    zero = squares == 0.0
    gain = jnp.where(
        zero, 0.0, COUPLE * jnp.exp(-SPREAD * squares) / jnp.where(zero, 1.0, squares)
    )
    loads["xf"].wait()
    loads["xi"].wait()
    for copy in x_copies:
        copy.wait_recv()
    spectrum = dot(local["xf"][...], xrec[...].reshape(ngy * 48, 128))
    urec[b] = dot(local["xi"][...], gain * spectrum)
    u_copies = [
        send(urec.at[b], urec.at[b], s_u.at[d], r_u.at[d], "gz", d) for d in range(1, ngz)
    ]
    started += u_copies

    for copy in side_copies:
        copy.wait()
    f0[0, 0:5] = f0[0, 0:5] + xrecv[0, 0]
    f0[1, 1:6] = f0[1, 1:6] + xrecv[0, 1]
    f0[0, 11:16] = f0[0, 11:16] + xrecv[1, 0]
    f0[1, 10:15] = f0[1, 10:15] + xrecv[1, 1]
    rims = [
        hp[q]
        + jnp.where(
            lane < 64, pltpu.roll(xhrecv[0, q], 64, 1), pltpu.roll(xhrecv[1, q], 64, 1)
        )
        for q in range(2)
    ]

    def unpack(plane, carry):
        by = 124 - 8 * plane
        by = jnp.where(by < 0, by + 128, by)
        for q in range(2):
            t1[q, plane] = jnp.where(edge, pltpu.roll(rims[q], by, 1), 0.0)
        return carry

    lax.fori_loop(0, WX, unpack, 0)
    window = [
        jnp.concatenate([f0[q].reshape(WX * WY, 128), t1[q].reshape(WX * WY, 128)], axis=1)
        for q in range(2)
    ]
    loads["sz"].wait()
    loads["an"].wait()

    def keep(target, slot, value):
        for k in range(3):
            target[slot, k] = value[:, 128 * k : 128 * (k + 1)].reshape(inner, WY, 128)

    smoothed = rdot(window[0], local["sz"][:, 0:384])
    keep(near, 0, dot(local["an"][0], smoothed))
    keep(near, 1, dot(local["an"][1], smoothed))
    keep(near, 2, dot(local["an"][2], rdot(window[0], local["sz"][:, 384:768])))
    keep(near, 3, -2.0 * dot(local["an"][2], rdot(window[1], local["sz"][:, 0:384])))

    loads["yi"].wait()
    for copy in u_copies:
        copy.wait_recv()
    wrec[c] = dot(local["yi"][...], urec[...].reshape(ngz * 48, 128))
    w_copies = [
        send(wrec.at[c], wrec.at[c], s_w.at[d], r_w.at[d], "gx", d) for d in range(1, ngx)
    ]
    started += w_copies

    def slopes(plane):
        rows = pl.ds(8, BY)
        weights = [wt[n, plane + 2, rows, :] for n in range(9)]
        slope = []
        for axis in range(3):
            shift = SMAX * bent[axis, plane]
            slope += [shift - 0.5, -2.0 * shift, shift + 0.5]
        return weights, slope

    def plus(total, term):
        return term if total is None else total + term

    def read(plane, carry):
        weights, slope = slopes(plane)
        pushes = [vals[axis, plane + 2, 8:24, :] for axis in range(3)]
        sums = [None] * 6
        for k in range(3):
            mid = [None] * 6
            for j in range(3):
                line = [None] * 5
                for i in range(3):
                    at = [near[q, k, plane + i, pl.ds(j, BY), :] for q in range(4)]
                    both = at[3]
                    for q in range(3):
                        line[q] = plus(line[q], weights[i] * at[q])
                        both = both + pushes[q] * at[q]
                    line[3] = plus(line[3], weights[i] * both)
                    line[4] = plus(line[4], slope[i] * both)
                for q in range(3):
                    mid[q] = plus(mid[q], weights[3 + j] * line[q])
                mid[3] = plus(mid[3], weights[3 + j] * line[4])
                mid[4] = plus(mid[4], slope[3 + j] * line[3])
                mid[5] = plus(mid[5], weights[3 + j] * line[3])
            for q in range(5):
                sums[q] = plus(sums[q], weights[6 + k] * mid[q])
            sums[5] = plus(sums[5], slope[6 + k] * mid[5])
        for q in range(6):
            part[q, plane] = sums[q]
        return carry

    lax.fori_loop(0, BX, read, 0)

    for name in ("zi", "uf", "up"):
        loads[name].wait()
    for copy in w_copies:
        copy.wait_recv()
    spread = rdot(jnp.concatenate([wrec[d] for d in range(ngx)], axis=1), local["zi"][...])
    value, slant = spread[:, 0:128], spread[:, 128:256]
    far = [
        dot(local["uf"][0], value),
        dot(local["uf"][1], value),
        dot(local["uf"][2], slant),
    ]
    fine = dot(local["up"][...], spread[:, 256:640])
    for k in range(3):
        psi[k] = fine[:, 128 * k : 128 * (k + 1)].reshape(inner, WY, 128)
    for axis in range(3):
        moved[axis] = SMAX * bent[axis] + STEP * (
            part[axis] + far[axis].reshape(BX, BY, 128)
        )

    def finish(plane, carry):
        weights, slope = slopes(plane)
        sums = [part[3 + axis, plane] for axis in range(3)]
        for k in range(3):
            mid = [None] * 3
            for j in range(3):
                line = [None] * 2
                for i in range(3):
                    at = psi[k, plane + i, pl.ds(j, BY), :]
                    line[0] = plus(line[0], weights[i] * at)
                    line[1] = plus(line[1], slope[i] * at)
                mid[0] = plus(mid[0], weights[3 + j] * line[1])
                mid[1] = plus(mid[1], slope[3 + j] * line[0])
                mid[2] = plus(mid[2], weights[3 + j] * line[0])
            sums[0] = sums[0] + weights[6 + k] * mid[0]
            sums[1] = sums[1] + weights[6 + k] * mid[1]
            sums[2] = sums[2] + slope[6 + k] * mid[2]
        for axis in range(3):
            bend = bent[axis, plane]
            grad[axis, plane] = (cot[axis, plane] + sums[axis]) * (SMAX * (1.0 - bend * bend))
        return carry

    lax.fori_loop(0, BX, finish, 0)
    for copy in started:
        copy.wait_send()


def body(tables, sizes, latent, cotangent):
    ngx, ngy, ngz = sizes
    dma = pltpu.SemaphoreType.DMA
    f32 = jnp.float32

    def vmem(*shape):
        return pltpu.VMEM(shape, f32)

    arrays = [jnp.asarray(tables[name]) for name in NAMES]
    locals_ = [
        pltpu.VMEM(array.shape[1:], array.dtype)
        for array in arrays
    ]
    scratch = [
        vmem(3, BX, BY, 128),
        vmem(9, 12, 32, 128),
        vmem(3, 12, 32, 128),
        vmem(9, 14, 40, 128),
        vmem(2, WX, WY, 128),
        vmem(2, WX, WY, 128),
        vmem(2, WY, 128),
        vmem(2, 2, WY, 128),
        vmem(2, 2, WY, 128),
        vmem(2, 2, 12, 8, 128),
        vmem(2, 2, 8, 128),
        vmem(2, 2, 5, WY, 128),
        vmem(2, 2, WY, 128),
        vmem(ngx, 64, 128),
        vmem(ngx, 64, 128),
        vmem(ngz, 48, 128),
        vmem(ngz, 48, 128),
        vmem(ngy, 48, 128),
        vmem(ngz, 48, 128),
        vmem(ngx, 64, 128),
        vmem(4, 3, BX + 2, WY, 128),
        vmem(3, BX + 2, WY, 128),
        vmem(6, BX, BY, 128),
        dma((len(NAMES),)),
        dma((ngx,)), dma((ngx,)),
        dma((ngz,)), dma((ngz,)),
        dma((ngz,)), dma((ngz,)),
        dma((ngx,)), dma((ngx,)),
        dma((ngy,)), dma((ngy,)),
        dma((12,)), dma((12,)),
    ]
    whole = pl.BlockSpec(memory_space=pltpu.VMEM)
    return pl.pallas_call(
        functools.partial(kernel, sizes),
        out_shape=[jax.ShapeDtypeStruct((3, BX, BY, BZ), f32)] * 2,
        in_specs=[whole, whole] + [pl.BlockSpec(memory_space=pl.ANY)] * len(NAMES),
        out_specs=[whole, whole],
        scratch_shapes=locals_ + scratch,
        compiler_params=pltpu.CompilerParams(
            collective_id=0, has_side_effects=True, vmem_limit_bytes=52 * 1024 * 1024
        ),
    )(latent, cotangent, *arrays)


def solution(mesh):
    sizes = (mesh.shape["gx"], mesh.shape["gy"], mesh.shape["gz"])
    tables = make_tables(*sizes)
    placed = P(None, "gy", "gz", "gx")
    return jax.shard_map(
        functools.partial(body, tables, sizes),
        mesh=mesh,
        in_specs=(placed, placed),
        out_specs=(placed, placed),
        check_vma=False,
    )
```

```python
import functools
import math

import jax
import jax.numpy as jnp
import ml_dtypes
import numpy as np
from jax import lax
from jax.experimental import pallas as pl
from jax.experimental.pallas import tpu as pltpu
from jax.sharding import PartitionSpec as P

SMAX = 0.45
STEP = 0.5
SHORT = 4.0
COUPLE = 0.5
SPREAD = 0.125
KERNEL = (0.05, 0.25, 0.4, 0.25, 0.05)
MESH = pl.DeviceIdType.MESH

BX, BY, BZ = 8, 16, 128
CX, CY, CZ = 4, 8, 64
WX, WY = 16, 24


def basis(length):
    n = np.arange(length)
    angle = 2.0 * np.pi * ((n[:, None] * n[None, :]) % length) / length
    return (np.cos(angle) + np.sin(angle)) / math.sqrt(length)


def five(delta):
    return np.where(np.abs(delta) <= 2, np.take(np.array(KERNEL), np.clip(delta + 2, 0, 4)), 0.0)


def same(left, right):
    return (left[:, None] == right[None, :]).astype(np.float64)


def central(left, right):
    return 0.5 * (same(left + 1, right) - same(left - 1, right))


def make_tables(ngx, ngy, ngz):
    mx, my, mz = CX * ngy, CY * ngz, CZ * ngx
    qx, qy, qz = basis(mx), basis(my), basis(mz)
    f = {}
    cxe, cye = np.arange(-1, CX + 1), np.arange(-1, CY + 1)
    fx, fy = np.arange(-1, BX + 1), np.arange(-4, BY + 4)
    ox, oy, oz = np.arange(BX), np.arange(BY), np.arange(BZ)
    down = lambda v: np.floor_divide(v, 2)

    def rows64(matrix):
        return np.concatenate([matrix, np.zeros((64 - matrix.shape[0], matrix.shape[1]))])

    f["cd"] = rows64(np.kron(same(cxe, down(fx)), same(cye, down(fy)) * ((fy >= -1) & (fy <= BY))))
    own_x, own_y = same(cxe, down(ox)), same(cye, down(oy))
    f["cp"] = rows64(
        np.concatenate(
            [
                np.kron(-central(cxe, down(ox)), own_y),
                np.kron(own_x, -central(cye, down(oy))),
                np.kron(own_x, own_y),
            ],
            axis=1,
        )
    )
    zt = np.zeros((ngx, 512, ngx, 2, CZ))
    for c in range(ngx):
        zc = CZ * c + down(oz)
        q = qz.reshape(mz, ngx, CZ)
        zt[c, 0:128, :, 0] = q[zc % mz]
        zt[c, 128, :, 0] = q[(CZ * c + CZ) % mz]
        zt[c, 255, :, 0] = q[(CZ * c - 1) % mz]
        zt[c, 256:384, :, 1] = q[zc % mz]
        zt[c, 384:512, :, 1] = 0.5 * (q[(zc + 1) % mz] - q[(zc - 1) % mz])
    f["zt"] = zt.reshape(ngx, 512, ngx * 128)
    yt = np.zeros((ngz, ngz, 6, CY, 64))
    for b in range(ngz):
        for x in range(6):
            for y in range(10):
                yt[b, :, x, :, x * 10 + y] = qy[(CY * b + y - 1) % my].reshape(ngz, CY)
    f["yt"] = yt.reshape(ngz, ngz * 48, 64)
    xf = np.zeros((mx, CY, ngy, 6, CY))
    xi = np.zeros((ngy, 6, CY, mx, CY))
    for a in range(ngy):
        for x in range(6):
            for m in range(CY):
                xf[:, m, a, x, m] = qx[(CX * a + x - 1) % mx]
                xi[a, x, m, :, m] = qx[(CX * a + x - 1) % mx]
    f["xf"] = xf.reshape(mx * CY, ngy * 48)
    f["xi"] = xi.reshape(ngy, 48, mx * CY)
    square = lambda total: 4.0 * np.sin(np.pi * np.arange(total) / total) ** 2
    ka = square(mx)[None, :, None] + square(my).reshape(ngz, 1, CY)
    f["ka"] = np.broadcast_to(ka.reshape(ngz, mx * CY, 1), (ngz, mx * CY, 128))
    kb = np.concatenate([square(mz).reshape(ngx, CZ)] * 2, axis=1)
    f["kb"] = np.broadcast_to(kb[:, None], (ngx, 8, 128))
    yi = np.zeros((ngz, 64, ngz, 6, CY))
    for b in range(ngz):
        for x in range(6):
            for y in range(10):
                yi[b, x * 10 + y, :, x, :] = qy[(CY * b + y - 1) % my].reshape(ngz, CY)
    f["yi"] = yi.reshape(ngz, 64, ngz * 48)
    beside = lambda node: down(node) + np.where(node % 2 == 0, -1, 1)
    zi = np.zeros((ngx, ngx, 2, CZ, 512))
    for c in range(ngx):
        at = lambda cell: qz[(CZ * c + cell) % mz].T.reshape(ngx, CZ, 128)
        zi[c, :, 0, :, 0:128] = at(down(oz))
        zi[c, :, 0, :, 128:256] = 0.5 * (at(down(oz) + 1) - at(down(oz) - 1))
        zi[c, :, 1, :, 256:384] = at(down(oz))
        zi[c, :, 1, :, 384:512] = at(beside(oz))
    f["zi"] = zi.reshape(ngx, ngx * 128, 512)
    pad4 = lambda matrix: np.concatenate([matrix, np.zeros((matrix.shape[0], 4))], axis=1)
    f["uf"] = np.stack(
        [
            pad4(np.kron(central(down(ox), cxe), same(down(oy), cye))),
            pad4(np.kron(same(down(ox), cxe), central(down(oy), cye))),
            pad4(np.kron(same(down(ox), cxe), same(down(oy), cye))),
        ]
    )
    ry = np.arange(-1, WY - 1)
    row = ((ry <= BY) * 1.0)[:, None]
    cells = (down, beside)
    f["up"] = pad4(
        np.concatenate(
            [np.kron(same(p(ox), cxe), same(q(oy), cye)) for p in cells for q in cells]
        )
    )
    zw = np.concatenate([oz, oz + 128])
    zw[252:256] = np.arange(-4, 0)
    valid = np.concatenate([np.ones(128), np.ones(4), np.zeros(120), np.ones(4)])[:, None]
    tap = lambda target, extra: five(target[None, :] + extra - zw[:, None]) * valid
    f["sz"] = np.concatenate(
        [tap(oz + k, 0) for k in (-1, 0, 1)]
        + [tap(oz + k, 1) - tap(oz + k, -1) for k in (-1, 0, 1)],
        axis=1,
    )
    wx, wy = np.arange(-4, WX - 4), np.arange(-4, WY - 4)
    kx = lambda extra: five(fx[:, None] + extra - wx[None, :])
    ky = lambda extra: five(ry[:, None] + extra - wy[None, :]) * row
    half = 0.5 * SHORT
    f["an"] = np.stack(
        [
            half * np.kron(kx(1) - kx(-1), ky(0)),
            half * np.kron(kx(0), ky(1) - ky(-1)),
            half * np.kron(kx(0), ky(0)),
        ]
    )
    f["cq"], f["c0"] = f["cp"][:, 0:256], f.pop("cp")[:, 256:384]
    tables = {}
    for name, value in f.items():
        if name not in AXIS_OF:
            value = value[None]
        value = value.astype(np.float32)
        if name in LEFT or name in RIGHT:
            high = value.astype(ml_dtypes.bfloat16)
            low = (value - high.astype(np.float32)).astype(ml_dtypes.bfloat16)
            value = np.concatenate([high, high, low], axis=-1 if name in LEFT else -2)
        least = -(-TABLE_BYTES // value[0].nbytes)
        filler = np.zeros((max(0, least - len(value)),) + value.shape[1:], value.dtype)
        tables[name] = np.ascontiguousarray(np.concatenate([value, filler]))
    return tables


TABLE_BYTES = 2**21
NAMES = (
    "cd", "cq", "c0", "zt", "yt", "xf", "xi", "ka", "kb", "yi", "sz", "an", "zi", "uf", "up",
)
LEFT = ("cd", "cq", "c0", "yt", "xf", "xi", "yi", "uf", "up", "an")
RIGHT = ("zt", "zi", "sz")


def halves(value):
    high = value.astype(jnp.bfloat16)
    low = (value - high.astype(jnp.float32)).astype(jnp.bfloat16)
    return high, low


def dot(table, value):
    high, low = halves(value)
    stacked = jnp.concatenate([high, low, high], axis=0)
    return jnp.dot(table, stacked, preferred_element_type=jnp.float32)


def rdot(value, table):
    high, low = halves(value)
    stacked = jnp.concatenate([high, low, high], axis=1)
    return jnp.dot(stacked, table, preferred_element_type=jnp.float32)


AXIS_OF = {"zt": "gx", "yt": "gz", "xi": "gy", "ka": "gz", "kb": "gx", "yi": "gz", "zi": "gx"}


def kernel(sizes, lat_hbm, cot_hbm, *refs):
    ngx, ngy, ngz = sizes
    tables = dict(zip(NAMES, refs[: len(NAMES)]))
    moved, grad = refs[len(NAMES) : len(NAMES) + 2]
    rest = refs[len(NAMES) + 2 :]
    local = dict(zip(NAMES, rest[: len(NAMES)]))
    (
        lat, cot, cell, bent, wt, vals, bk, f0, t1, hp, tsend, trecv, yrecv, yhrecv, xrecv, xhrecv,
        zbuf, zrecv, ybuf, yrec, xrec, urec, wrec, near, psi, part,
        table_sem, arg_sem, s_z, r_z, s_y, r_y, s_u, r_u, s_w, r_w, s_x, r_x, s_h, r_h,
    ) = rest[len(NAMES) :]
    c, a, b = lax.axis_index("gx"), lax.axis_index("gy"), lax.axis_index("gz")
    place = {"gx": c, "gy": a, "gz": b}
    size = {"gx": ngx, "gy": ngy, "gz": ngz}

    def other(axis, step):
        return {axis: lax.rem(place[axis] + step, size[axis])}

    arguments = [
        pltpu.make_async_copy(lat_hbm, lat, arg_sem.at[0]),
        pltpu.make_async_copy(cot_hbm, cot, arg_sem.at[1]),
    ]
    for copy in arguments:
        copy.start()
    barrier = pltpu.get_barrier_semaphore()
    partners = [(axis, step) for axis in size for step in range(1, size[axis])]
    for axis, step in partners:
        pl.semaphore_signal(barrier, inc=1, device_id=other(axis, step), device_id_type=MESH)
    loads = {}
    for number, name in enumerate(NAMES):
        source = tables[name].at[place[AXIS_OF[name]] if name in AXIS_OF else 0]
        loads[name] = pltpu.make_async_copy(source, local[name], table_sem.at[number])
        loads[name].start()

    started = []

    def send(source, target, send_sem, recv_sem, axis, step):
        copy = pltpu.make_async_remote_copy(
            src_ref=source,
            dst_ref=target,
            send_sem=send_sem,
            recv_sem=recv_sem,
            device_id=other(axis, step),
            device_id_type=MESH,
        )
        copy.start()
        return copy

    lane = lax.broadcasted_iota(jnp.int32, (WY, 128), 1)
    edge = jnp.logical_or(lane < 4, lane >= 124)
    upper = lax.rem(lane, 8) >= 4

    wt[...] = jnp.zeros_like(wt)
    arguments[0].wait()
    for axis in range(3):
        bend = jnp.tanh(lat[axis])
        bent[axis] = bend
        shift = SMAX * bend
        wt[3 * axis, 2:10, 8:24] = 0.5 * (0.5 - shift) ** 2
        wt[3 * axis + 1, 2:10, 8:24] = 0.75 - shift * shift
        wt[3 * axis + 2, 2:10, 8:24] = 0.5 * (0.5 + shift) ** 2

    def gathered(plane, charges):
        totals = [[None] * 3 for _ in range(charges or 1)]
        for i in range(3):
            at = plane + 2 - i
            for j in range(3):
                rows = pl.ds(5 - j, WY)
                cross = wt[i, at, rows, :] * wt[3 + j, at, rows, :]
                for k in range(3):
                    weight = cross * wt[6 + k, at, rows, :]
                    for q in range(charges or 1):
                        term = weight * vals[q, at, rows, :] if charges else weight
                        totals[q][k] = term if totals[q][k] is None else totals[q][k] + term
        return totals

    def paint(plane, carry):
        ((low, middle, high),) = gathered(plane, 0)
        low = pltpu.roll(low, 127, 1)
        high = pltpu.roll(high, 1, 1)
        keep_low, keep_high = lane < 127, lane >= 1
        main = middle + jnp.where(keep_low, low, 0.0) + jnp.where(keep_high, high, 0.0)
        spill = jnp.where(keep_low, 0.0, low) + jnp.where(keep_high, 0.0, high)
        f0[0, plane + 3] = main
        t1[0, plane + 3] = spill
        return carry

    lax.fori_loop(0, BX + 2, paint, 0)

    loads["cd"].wait()
    loads["cq"].wait()
    loads["c0"].wait()
    inner = BX + 2
    density = jnp.concatenate(
        [f0[0, 3:13].reshape(inner * WY, 128), t1[0, 3:13].reshape(inner * WY, 128)], axis=1
    )
    rho = dot(local["cd"][...], density)
    arguments[1].wait()
    pushed = [(STEP * cot[axis]).reshape(BX * BY, 128) for axis in range(3)]
    cross_source = dot(local["cq"][...], jnp.concatenate(pushed[:2], axis=0))
    along_source = dot(local["c0"][...], pushed[2])
    loads["zt"].wait()
    modes = rdot(jnp.concatenate([rho, cross_source, along_source], axis=1), local["zt"][...])
    for j in range(ngx):
        zbuf[j] = modes[:, 128 * j : 128 * (j + 1)]
    pl.semaphore_wait(barrier, len(partners))
    z_copies = [
        send(zbuf.at[lax.rem(c + d, ngx)], zrecv.at[d], s_z.at[d], r_z.at[d], "gx", d)
        for d in range(1, ngx)
    ]
    started += z_copies

    f0[0, 0:3] = jnp.zeros((3, WY, 128), jnp.float32)
    f0[0, 13:16] = jnp.zeros((3, WY, 128), jnp.float32)
    t1[0, 0:3] = jnp.zeros((3, WY, 128), jnp.float32)
    t1[0, 13:16] = jnp.zeros((3, WY, 128), jnp.float32)
    f0[1] = jnp.zeros((WX, WY, 128), jnp.float32)
    t1[1] = jnp.zeros((WX, WY, 128), jnp.float32)
    vals[...] = jnp.zeros_like(vals)
    bk[...] = jnp.zeros_like(bk)
    for axis in range(3):
        vals[axis, 2:10, 8:24] = STEP * cot[axis]

    def paint_back(plane, carry):
        totals = gathered(plane, 3)
        for q in range(3):
            for k in range(3):
                bk[3 * q + k, plane + 2, 8:32, :] = totals[q][k]
        return carry

    lax.fori_loop(0, BX + 2, paint_back, 0)

    def spread_back(plane, carry):
        at = plane + 1

        def cross(k):
            return 0.5 * (
                bk[k, at + 1, 8:32, :] - bk[k, at - 1, 8:32, :]
                + bk[3 + k, at, 9:33, :] - bk[3 + k, at, 7:31, :]
            )

        up = [0.5 * bk[6 + k, at, 8:32, :] for k in range(3)]
        parts = {
            -2: up[0],
            -1: cross(0) + up[1],
            1: cross(2) - up[1],
            2: -up[2],
        }
        main = cross(1) + up[2] - up[0]
        spill = None
        for step, value in parts.items():
            rolled = pltpu.roll(value, step % 128, 1)
            keep = lane >= step if step > 0 else lane < 128 + step
            main = main + jnp.where(keep, rolled, 0.0)
            over = jnp.where(keep, 0.0, rolled)
            spill = over if spill is None else spill + over
        f0[1, plane + 2] = main
        t1[1, plane + 2] = spill
        return carry

    lax.fori_loop(0, BX + 4, spread_back, 0)

    def pack(plane, carry):
        by = 8 * plane + 4
        out = []
        for q in range(2):
            out.append(carry[2 * q] + pltpu.roll(jnp.where(edge, f0[q, plane], 0.0), by, 1))
            out.append(carry[2 * q + 1] + pltpu.roll(t1[q, plane], by, 1))
        return tuple(out)

    empty = jnp.zeros((WY, 128), jnp.float32)
    packed = lax.fori_loop(2, BX + 6, pack, (empty,) * 4)
    for q in range(2):
        face, spill = packed[2 * q], packed[2 * q + 1]
        tsend[0, q] = jnp.where(upper, spill, face)
        tsend[1, q] = jnp.where(upper, face, spill)
        hp[q] = spill
    t_copies = [
        send(tsend.at[0], trecv.at[0], s_h.at[0], r_h.at[0], "gx", 1),
        send(tsend.at[1], trecv.at[1], s_h.at[1], r_h.at[1], "gx", ngx - 1),
    ]
    started += t_copies

    for copy in z_copies:
        copy.wait_recv()
    total = zbuf[c]
    for d in range(1, ngx):
        total = total + zrecv[d]
    loads["yt"].wait()
    ybuf[...] = dot(local["yt"][...], total).reshape(ngz, 48, 128)
    y_copies = [
        send(ybuf.at[lax.rem(b + d, ngz)], yrec.at[d], s_y.at[d], r_y.at[d], "gz", d)
        for d in range(1, ngz)
    ]
    started += y_copies

    for copy in t_copies:
        copy.wait_recv()
    fixes = []
    for q in range(2):
        from_left, from_right = trecv[0, q], trecv[1, q]
        hp[q] = hp[q] + jnp.where(upper, from_right, from_left)
        fixes.append(jnp.where(upper, from_left, from_right))

    def fix(plane, carry):
        by = 124 - 8 * plane
        by = jnp.where(by < 0, by + 128, by)
        for q in range(2):
            f0[q, plane] = f0[q, plane] + jnp.where(edge, pltpu.roll(fixes[q], by, 1), 0.0)
        return carry

    lax.fori_loop(2, BX + 6, fix, 0)
    rim_copies = [
        send(f0.at[:, 2:14, 16:24], yrecv.at[0], s_h.at[2], r_h.at[2], "gz", 1),
        send(f0.at[:, 2:14, 0:8], yrecv.at[1], s_h.at[3], r_h.at[3], "gz", ngz - 1),
        send(hp.at[:, 16:24], yhrecv.at[0], s_h.at[4], r_h.at[4], "gz", 1),
        send(hp.at[:, 0:8], yhrecv.at[1], s_h.at[5], r_h.at[5], "gz", ngz - 1),
    ]

    for copy in y_copies:
        copy.wait_recv()
    total = ybuf[b]
    for d in range(1, ngz):
        total = total + yrec[d]
    xrec[a] = total
    x_copies = [
        send(xrec.at[a], xrec.at[a], s_x.at[d], r_x.at[d], "gy", d) for d in range(1, ngy)
    ]
    started += x_copies

    for copy in rim_copies:
        copy.wait()
    f0[:, 2:14, 0:8] = f0[:, 2:14, 0:8] + yrecv[0]
    f0[:, 2:14, 16:24] = f0[:, 2:14, 16:24] + yrecv[1]
    hp[:, 0:8] = hp[:, 0:8] + yhrecv[0]
    hp[:, 16:24] = hp[:, 16:24] + yhrecv[1]
    side_copies = [
        send(f0.at[0, 8:13], xrecv.at[0, 0], s_h.at[6], r_h.at[6], "gy", 1),
        send(f0.at[1, 9:14], xrecv.at[0, 1], s_h.at[7], r_h.at[7], "gy", 1),
        send(f0.at[0, 3:8], xrecv.at[1, 0], s_h.at[8], r_h.at[8], "gy", ngy - 1),
        send(f0.at[1, 2:7], xrecv.at[1, 1], s_h.at[9], r_h.at[9], "gy", ngy - 1),
        send(hp, xhrecv.at[0], s_h.at[10], r_h.at[10], "gy", 1),
        send(hp, xhrecv.at[1], s_h.at[11], r_h.at[11], "gy", ngy - 1),
    ]

    loads["ka"].wait()
    loads["kb"].wait()
    squares = local["ka"][...] + local["kb"][0:1, :]
    zero = squares == 0.0
    gain = jnp.where(
        zero, 0.0, COUPLE * jnp.exp(-SPREAD * squares) / jnp.where(zero, 1.0, squares)
    )
    loads["xf"].wait()
    loads["xi"].wait()
    for copy in x_copies:
        copy.wait_recv()
    spectrum = dot(local["xf"][...], xrec[...].reshape(ngy * 48, 128))
    urec[b] = dot(local["xi"][...], gain * spectrum)
    u_copies = [
        send(urec.at[b], urec.at[b], s_u.at[d], r_u.at[d], "gz", d) for d in range(1, ngz)
    ]
    started += u_copies

    loads["yi"].wait()
    for copy in u_copies:
        copy.wait_recv()
    wrec[c] = dot(local["yi"][...], urec[...].reshape(ngz * 48, 128))
    w_copies = [
        send(wrec.at[c], wrec.at[c], s_w.at[d], r_w.at[d], "gx", d) for d in range(1, ngx)
    ]
    started += w_copies

    for copy in side_copies:
        copy.wait()
    f0[0, 0:5] = f0[0, 0:5] + xrecv[0, 0]
    f0[1, 1:6] = f0[1, 1:6] + xrecv[0, 1]
    f0[0, 11:16] = f0[0, 11:16] + xrecv[1, 0]
    f0[1, 10:15] = f0[1, 10:15] + xrecv[1, 1]
    rims = [
        hp[q]
        + jnp.where(
            lane < 64, pltpu.roll(xhrecv[0, q], 64, 1), pltpu.roll(xhrecv[1, q], 64, 1)
        )
        for q in range(2)
    ]

    def unpack(plane, carry):
        by = 124 - 8 * plane
        by = jnp.where(by < 0, by + 128, by)
        for q in range(2):
            t1[q, plane] = jnp.where(edge, pltpu.roll(rims[q], by, 1), 0.0)
        return carry

    lax.fori_loop(0, WX, unpack, 0)
    window = [
        jnp.concatenate([f0[q].reshape(WX * WY, 128), t1[q].reshape(WX * WY, 128)], axis=1)
        for q in range(2)
    ]
    loads["sz"].wait()
    loads["an"].wait()

    def keep(target, slot, value):
        for k in range(3):
            target[slot, k] = value[:, 128 * k : 128 * (k + 1)].reshape(inner, WY, 128)

    smoothed = rdot(window[0], local["sz"][:, 0:384])
    keep(near, 0, dot(local["an"][0], smoothed))
    keep(near, 1, dot(local["an"][1], smoothed))
    keep(near, 2, dot(local["an"][2], rdot(window[0], local["sz"][:, 384:768])))
    keep(near, 3, -2.0 * dot(local["an"][2], rdot(window[1], local["sz"][:, 0:384])))

    def slopes(plane):
        rows = pl.ds(8, BY)
        weights = [wt[n, plane + 2, rows, :] for n in range(9)]
        slope = []
        for axis in range(3):
            shift = SMAX * bent[axis, plane]
            slope += [shift - 0.5, -2.0 * shift, shift + 0.5]
        return weights, slope

    def plus(total, term):
        return term if total is None else total + term

    even_row = lax.rem(lax.broadcasted_iota(jnp.int32, (BY, 128), 0), 2) == 0
    even_lane = lax.rem(lax.broadcasted_iota(jnp.int32, (BY, 128), 1), 2) == 0

    def read(plane, carry):
        weights, slope = slopes(plane)
        pushes = [vals[axis, plane + 2, 8:24, :] for axis in range(3)]
        sums = [None] * 6
        for k in range(3):
            mid = [None] * 6
            for j in range(3):
                line = [None] * 5
                for i in range(3):
                    at = [near[q, k, plane + i, pl.ds(j, BY), :] for q in range(4)]
                    both = at[3]
                    for q in range(3):
                        line[q] = plus(line[q], weights[i] * at[q])
                        both = both + pushes[q] * at[q]
                    line[3] = plus(line[3], weights[i] * both)
                    line[4] = plus(line[4], slope[i] * both)
                for q in range(3):
                    mid[q] = plus(mid[q], weights[3 + j] * line[q])
                mid[3] = plus(mid[3], weights[3 + j] * line[4])
                mid[4] = plus(mid[4], slope[3 + j] * line[3])
                mid[5] = plus(mid[5], weights[3 + j] * line[3])
            for q in range(5):
                sums[q] = plus(sums[q], weights[6 + k] * mid[q])
            sums[5] = plus(sums[5], slope[6 + k] * mid[5])
        for q in range(6):
            part[q, plane] = sums[q]
        even = (lax.rem(plane, 2) == 0, even_row, even_lane)
        for axis in range(3):
            for n, (low, mid, high) in enumerate(
                (weights[3 * axis : 3 * axis + 3], slope[3 * axis : 3 * axis + 3])
            ):
                cell[4 * axis + 2 * n, plane] = mid + jnp.where(even[axis], high, low)
                cell[4 * axis + 2 * n + 1, plane] = jnp.where(even[axis], low, high)
        return carry

    lax.fori_loop(0, BX, read, 0)

    for name in ("zi", "uf", "up"):
        loads[name].wait()
    for copy in w_copies:
        copy.wait_recv()
    spread = rdot(jnp.concatenate([wrec[d] for d in range(ngx)], axis=1), local["zi"][...])
    value, slant = spread[:, 0:128], spread[:, 128:256]
    far = [
        dot(local["uf"][0], value),
        dot(local["uf"][1], value),
        dot(local["uf"][2], slant),
    ]
    fine = dot(local["up"][...], spread[:, 256:512])
    for k in range(2):
        psi[k] = fine[:, 128 * k : 128 * (k + 1)].reshape(4, BX, BY, 128)
    for axis in range(3):
        moved[axis] = SMAX * bent[axis] + STEP * (
            part[axis] + far[axis].reshape(BX, BY, 128)
        )

    def finish(plane, carry):
        sums = [part[3 + axis, plane] for axis in range(3)]
        group = [cell[n, plane] for n in range(12)]
        for k in range(2):
            mid = [None] * 3
            for j in range(2):
                here, there = psi[k, j, plane], psi[k, 2 + j, plane]
                line = group[0] * here + group[1] * there
                tilt = group[2] * here + group[3] * there
                mid[0] = plus(mid[0], group[4 + j] * tilt)
                mid[1] = plus(mid[1], group[6 + j] * line)
                mid[2] = plus(mid[2], group[4 + j] * line)
            sums[0] = sums[0] + group[8 + k] * mid[0]
            sums[1] = sums[1] + group[8 + k] * mid[1]
            sums[2] = sums[2] + group[10 + k] * mid[2]
        for axis in range(3):
            bend = bent[axis, plane]
            grad[axis, plane] = (cot[axis, plane] + sums[axis]) * (SMAX * (1.0 - bend * bend))
        return carry

    lax.fori_loop(0, BX, finish, 0)
    for copy in started:
        copy.wait_send()


def body(tables, sizes, latent, cotangent):
    ngx, ngy, ngz = sizes
    dma = pltpu.SemaphoreType.DMA
    f32 = jnp.float32

    def vmem(*shape):
        return pltpu.VMEM(shape, f32)

    arrays = [jnp.asarray(tables[name]) for name in NAMES]
    locals_ = [
        pltpu.VMEM(array.shape[1:], array.dtype)
        for array in arrays
    ]
    scratch = [
        vmem(3, BX, BY, 128),
        vmem(3, BX, BY, 128),
        vmem(12, BX, BY, 128),
        vmem(3, BX, BY, 128),
        vmem(9, 12, 32, 128),
        vmem(3, 12, 32, 128),
        vmem(9, 14, 40, 128),
        vmem(2, WX, WY, 128),
        vmem(2, WX, WY, 128),
        vmem(2, WY, 128),
        vmem(2, 2, WY, 128),
        vmem(2, 2, WY, 128),
        vmem(2, 2, 12, 8, 128),
        vmem(2, 2, 8, 128),
        vmem(2, 2, 5, WY, 128),
        vmem(2, 2, WY, 128),
        vmem(ngx, 64, 128),
        vmem(ngx, 64, 128),
        vmem(ngz, 48, 128),
        vmem(ngz, 48, 128),
        vmem(ngy, 48, 128),
        vmem(ngz, 48, 128),
        vmem(ngx, 64, 128),
        vmem(4, 3, BX + 2, WY, 128),
        vmem(2, 4, BX, BY, 128),
        vmem(6, BX, BY, 128),
        dma((len(NAMES),)),
        dma((2,)),
        dma((ngx,)), dma((ngx,)),
        dma((ngz,)), dma((ngz,)),
        dma((ngz,)), dma((ngz,)),
        dma((ngx,)), dma((ngx,)),
        dma((ngy,)), dma((ngy,)),
        dma((12,)), dma((12,)),
    ]
    whole = pl.BlockSpec(memory_space=pltpu.VMEM)
    return pl.pallas_call(
        functools.partial(kernel, sizes),
        out_shape=[jax.ShapeDtypeStruct((3, BX, BY, BZ), f32)] * 2,
        in_specs=[pl.BlockSpec(memory_space=pl.ANY)] * (2 + len(NAMES)),
        out_specs=[whole, whole],
        scratch_shapes=locals_ + scratch,
        compiler_params=pltpu.CompilerParams(
            collective_id=0, has_side_effects=True, vmem_limit_bytes=54784 * 1024
        ),
    )(latent, cotangent, *arrays)


def solution(mesh):
    sizes = (mesh.shape["gx"], mesh.shape["gy"], mesh.shape["gz"])
    tables = make_tables(*sizes)
    placed = P(None, "gy", "gz", "gx")
    return jax.shard_map(
        functools.partial(body, tables, sizes),
        mesh=mesh,
        in_specs=(placed, placed),
        out_specs=(placed, placed),
        check_vma=False,
    )
```

```python
import functools
import math

import jax
import jax.numpy as jnp
import ml_dtypes
import numpy as np
from jax import lax
from jax.experimental import pallas as pl
from jax.experimental.pallas import tpu as pltpu
from jax.sharding import PartitionSpec as P

SMAX = 0.45
STEP = 0.5
SHORT = 4.0
COUPLE = 0.5
SPREAD = 0.125
KERNEL = (0.05, 0.25, 0.4, 0.25, 0.05)
MESH = pl.DeviceIdType.MESH

BX, BY, BZ = 8, 16, 128
CX, CY, CZ = 4, 8, 64
WX, WY = 16, 24


def basis(length):
    n = np.arange(length)
    angle = 2.0 * np.pi * ((n[:, None] * n[None, :]) % length) / length
    return (np.cos(angle) + np.sin(angle)) / math.sqrt(length)


def five(delta):
    return np.where(np.abs(delta) <= 2, np.take(np.array(KERNEL), np.clip(delta + 2, 0, 4)), 0.0)


def same(left, right):
    return (left[:, None] == right[None, :]).astype(np.float64)


def central(left, right):
    return 0.5 * (same(left + 1, right) - same(left - 1, right))


def make_tables(ngx, ngy, ngz):
    mx, my, mz = CX * ngy, CY * ngz, CZ * ngx
    qx, qy, qz = basis(mx), basis(my), basis(mz)
    f = {}
    cxe, cye = np.arange(-1, CX + 1), np.arange(-1, CY + 1)
    fx, fy = np.arange(-1, BX + 1), np.arange(-4, BY + 4)
    ox, oy, oz = np.arange(BX), np.arange(BY), np.arange(BZ)
    down = lambda v: np.floor_divide(v, 2)

    def rows64(matrix):
        return np.concatenate([matrix, np.zeros((64 - matrix.shape[0], matrix.shape[1]))])

    f["cd"] = rows64(np.kron(same(cxe, down(fx)), same(cye, down(fy)) * ((fy >= -1) & (fy <= BY))))
    own_x, own_y = same(cxe, down(ox)), same(cye, down(oy))
    f["cp"] = rows64(
        np.concatenate(
            [
                np.kron(-central(cxe, down(ox)), own_y),
                np.kron(own_x, -central(cye, down(oy))),
                np.kron(own_x, own_y),
            ],
            axis=1,
        )
    )
    zt = np.zeros((ngx, 512, ngx, 2, CZ))
    for c in range(ngx):
        zc = CZ * c + down(oz)
        q = qz.reshape(mz, ngx, CZ)
        zt[c, 0:128, :, 0] = q[zc % mz]
        zt[c, 128, :, 0] = q[(CZ * c + CZ) % mz]
        zt[c, 255, :, 0] = q[(CZ * c - 1) % mz]
        zt[c, 256:384, :, 1] = q[zc % mz]
        zt[c, 384:512, :, 1] = 0.5 * (q[(zc + 1) % mz] - q[(zc - 1) % mz])
    f["zt"] = zt.reshape(ngx, 512, ngx * 128)
    yt = np.zeros((ngz, ngz, 6, CY, 64))
    for b in range(ngz):
        for x in range(6):
            for y in range(10):
                yt[b, :, x, :, x * 10 + y] = qy[(CY * b + y - 1) % my].reshape(ngz, CY)
    f["yt"] = yt.reshape(ngz, ngz * 48, 64)
    xf = np.zeros((mx, CY, ngy, 6, CY))
    xi = np.zeros((ngy, 6, CY, mx, CY))
    for a in range(ngy):
        for x in range(6):
            for m in range(CY):
                xf[:, m, a, x, m] = qx[(CX * a + x - 1) % mx]
                xi[a, x, m, :, m] = qx[(CX * a + x - 1) % mx]
    f["xf"] = xf.reshape(mx * CY, ngy * 48)
    f["xi"] = xi.reshape(ngy, 48, mx * CY)
    square = lambda total: 4.0 * np.sin(np.pi * np.arange(total) / total) ** 2
    ka = square(mx)[None, :, None] + square(my).reshape(ngz, 1, CY)
    f["ka"] = np.broadcast_to(ka.reshape(ngz, mx * CY, 1), (ngz, mx * CY, 128))
    kb = np.concatenate([square(mz).reshape(ngx, CZ)] * 2, axis=1)
    f["kb"] = np.broadcast_to(kb[:, None], (ngx, 8, 128))
    yi = np.zeros((ngz, 64, ngz, 6, CY))
    for b in range(ngz):
        for x in range(6):
            for y in range(10):
                yi[b, x * 10 + y, :, x, :] = qy[(CY * b + y - 1) % my].reshape(ngz, CY)
    f["yi"] = yi.reshape(ngz, 64, ngz * 48)
    beside = lambda node: down(node) + np.where(node % 2 == 0, -1, 1)
    zi = np.zeros((ngx, ngx, 2, CZ, 512))
    for c in range(ngx):
        at = lambda cell: qz[(CZ * c + cell) % mz].T.reshape(ngx, CZ, 128)
        zi[c, :, 0, :, 0:128] = at(down(oz))
        zi[c, :, 0, :, 128:256] = 0.5 * (at(down(oz) + 1) - at(down(oz) - 1))
        zi[c, :, 1, :, 256:384] = at(down(oz))
        zi[c, :, 1, :, 384:512] = at(beside(oz))
    f["zi"] = zi.reshape(ngx, ngx * 128, 512)
    pad4 = lambda matrix: np.concatenate([matrix, np.zeros((matrix.shape[0], 4))], axis=1)
    f["uf"] = np.stack(
        [
            pad4(np.kron(central(down(ox), cxe), same(down(oy), cye))),
            pad4(np.kron(same(down(ox), cxe), central(down(oy), cye))),
            pad4(np.kron(same(down(ox), cxe), same(down(oy), cye))),
        ]
    )
    ry = np.arange(-1, WY - 1)
    row = ((ry <= BY) * 1.0)[:, None]
    cells = (down, beside)
    f["up"] = pad4(
        np.concatenate(
            [np.kron(same(p(ox), cxe), same(q(oy), cye)) for p in cells for q in cells]
        )
    )
    zw = np.concatenate([oz, oz + 128])
    zw[252:256] = np.arange(-4, 0)
    valid = np.concatenate([np.ones(128), np.ones(4), np.zeros(120), np.ones(4)])[:, None]
    tap = lambda target, extra: five(target[None, :] + extra - zw[:, None]) * valid
    own, past = oz, np.where(oz == 0, BZ, -1)
    ends = np.logical_or(oz == 0, oz == BZ - 1)[None, :]
    f["sz"] = np.concatenate(
        [tap(own, 0), tap(past, 0) * ends]
        + [tap(own, 1) - tap(own, -1), (tap(past, 1) - tap(past, -1)) * ends],
        axis=1,
    )
    wx, wy = np.arange(-4, WX - 4), np.arange(-4, WY - 4)
    kx = lambda extra: five(fx[:, None] + extra - wx[None, :])
    ky = lambda extra: five(ry[:, None] + extra - wy[None, :]) * row
    half = 0.5 * SHORT
    f["an"] = np.stack(
        [
            half * np.kron(kx(1) - kx(-1), ky(0)),
            half * np.kron(kx(0), ky(1) - ky(-1)),
            half * np.kron(kx(0), ky(0)),
        ]
    )
    f["cq"], f["c0"] = f["cp"][:, 0:256], f.pop("cp")[:, 256:384]
    tables = {}
    for name, value in f.items():
        if name not in AXIS_OF:
            value = value[None]
        value = value.astype(np.float32)
        if name in LEFT or name in RIGHT:
            high = value.astype(ml_dtypes.bfloat16)
            low = (value - high.astype(np.float32)).astype(ml_dtypes.bfloat16)
            value = np.concatenate([high, high, low], axis=-1 if name in LEFT else -2)
        least = -(-TABLE_BYTES // value[0].nbytes)
        filler = np.zeros((max(0, least - len(value)),) + value.shape[1:], value.dtype)
        tables[name] = np.ascontiguousarray(np.concatenate([value, filler]))
    return tables


TABLE_BYTES = 2**21
NAMES = (
    "cd", "cq", "c0", "zt", "yt", "xf", "xi", "ka", "kb", "yi", "sz", "an", "zi", "uf", "up",
)
LEFT = ("cd", "cq", "c0", "yt", "xf", "xi", "yi", "uf", "up", "an")
RIGHT = ("zt", "zi", "sz")


def halves(value):
    high = value.astype(jnp.bfloat16)
    low = (value - high.astype(jnp.float32)).astype(jnp.bfloat16)
    return high, low


def dot(table, value):
    high, low = halves(value)
    stacked = jnp.concatenate([high, low, high], axis=0)
    return jnp.dot(table, stacked, preferred_element_type=jnp.float32)


def rdot(value, table):
    high, low = halves(value)
    stacked = jnp.concatenate([high, low, high], axis=1)
    return jnp.dot(stacked, table, preferred_element_type=jnp.float32)


AXIS_OF = {"zt": "gx", "yt": "gz", "xi": "gy", "ka": "gz", "kb": "gx", "yi": "gz", "zi": "gx"}


def kernel(sizes, lat_hbm, cot_hbm, *refs):
    ngx, ngy, ngz = sizes
    tables = dict(zip(NAMES, refs[: len(NAMES)]))
    moved, grad = refs[len(NAMES) : len(NAMES) + 2]
    rest = refs[len(NAMES) + 2 :]
    local = dict(zip(NAMES, rest[: len(NAMES)]))
    (
        lat, cot, cell, bent, wt, vals, bk, f0, t1, hp, tsend, trecv, yrecv, yhrecv, xrecv, xhrecv,
        zbuf, zrecv, ybuf, yrec, xrec, urec, wrec, near, psi, part,
        table_sem, arg_sem, s_z, r_z, s_y, r_y, s_u, r_u, s_w, r_w, s_x, r_x, s_h, r_h,
    ) = rest[len(NAMES) :]
    c, a, b = lax.axis_index("gx"), lax.axis_index("gy"), lax.axis_index("gz")
    place = {"gx": c, "gy": a, "gz": b}
    size = {"gx": ngx, "gy": ngy, "gz": ngz}

    def other(axis, step):
        return {axis: lax.rem(place[axis] + step, size[axis])}

    arguments = [
        pltpu.make_async_copy(lat_hbm, lat, arg_sem.at[0]),
        pltpu.make_async_copy(cot_hbm, cot, arg_sem.at[1]),
    ]
    for copy in arguments:
        copy.start()
    barrier = pltpu.get_barrier_semaphore()
    partners = [(axis, step) for axis in size for step in range(1, size[axis])]
    for axis, step in partners:
        pl.semaphore_signal(barrier, inc=1, device_id=other(axis, step), device_id_type=MESH)
    loads = {}
    for number, name in enumerate(NAMES):
        source = tables[name].at[place[AXIS_OF[name]] if name in AXIS_OF else 0]
        loads[name] = pltpu.make_async_copy(source, local[name], table_sem.at[number])
        loads[name].start()

    started = []

    def send(source, target, send_sem, recv_sem, axis, step):
        copy = pltpu.make_async_remote_copy(
            src_ref=source,
            dst_ref=target,
            send_sem=send_sem,
            recv_sem=recv_sem,
            device_id=other(axis, step),
            device_id_type=MESH,
        )
        copy.start()
        return copy

    lane = lax.broadcasted_iota(jnp.int32, (WY, 128), 1)
    edge = jnp.logical_or(lane < 4, lane >= 124)
    upper = lax.rem(lane, 8) >= 4

    wt[...] = jnp.zeros_like(wt)
    arguments[0].wait()
    for axis in range(3):
        bend = jnp.tanh(lat[axis])
        bent[axis] = bend
        shift = SMAX * bend
        wt[3 * axis, 2:10, 8:24] = 0.5 * (0.5 - shift) ** 2
        wt[3 * axis + 1, 2:10, 8:24] = 0.75 - shift * shift
        wt[3 * axis + 2, 2:10, 8:24] = 0.5 * (0.5 + shift) ** 2

    def gathered(plane, charges):
        totals = [[None] * 3 for _ in range(charges or 1)]
        for i in range(3):
            at = plane + 2 - i
            for j in range(3):
                rows = pl.ds(5 - j, WY)
                cross = wt[i, at, rows, :] * wt[3 + j, at, rows, :]
                for k in range(3):
                    weight = cross * wt[6 + k, at, rows, :]
                    for q in range(charges or 1):
                        term = weight * vals[q, at, rows, :] if charges else weight
                        totals[q][k] = term if totals[q][k] is None else totals[q][k] + term
        return totals

    def paint(plane, carry):
        ((low, middle, high),) = gathered(plane, 0)
        low = pltpu.roll(low, 127, 1)
        high = pltpu.roll(high, 1, 1)
        keep_low, keep_high = lane < 127, lane >= 1
        main = middle + jnp.where(keep_low, low, 0.0) + jnp.where(keep_high, high, 0.0)
        spill = jnp.where(keep_low, 0.0, low) + jnp.where(keep_high, 0.0, high)
        f0[0, plane + 3] = main
        t1[0, plane + 3] = spill
        return carry

    lax.fori_loop(0, BX + 2, paint, 0)

    loads["cd"].wait()
    loads["cq"].wait()
    loads["c0"].wait()
    inner = BX + 2
    density = jnp.concatenate(
        [f0[0, 3:13].reshape(inner * WY, 128), t1[0, 3:13].reshape(inner * WY, 128)], axis=1
    )
    rho = dot(local["cd"][...], density)
    arguments[1].wait()
    pushed = [(STEP * cot[axis]).reshape(BX * BY, 128) for axis in range(3)]
    cross_source = dot(local["cq"][...], jnp.concatenate(pushed[:2], axis=0))
    along_source = dot(local["c0"][...], pushed[2])
    loads["zt"].wait()
    modes = rdot(jnp.concatenate([rho, cross_source, along_source], axis=1), local["zt"][...])
    for j in range(ngx):
        zbuf[j] = modes[:, 128 * j : 128 * (j + 1)]
    pl.semaphore_wait(barrier, len(partners))
    z_copies = [
        send(zbuf.at[lax.rem(c + d, ngx)], zrecv.at[d], s_z.at[d], r_z.at[d], "gx", d)
        for d in range(1, ngx)
    ]
    started += z_copies

    f0[0, 0:3] = jnp.zeros((3, WY, 128), jnp.float32)
    f0[0, 13:16] = jnp.zeros((3, WY, 128), jnp.float32)
    t1[0, 0:3] = jnp.zeros((3, WY, 128), jnp.float32)
    t1[0, 13:16] = jnp.zeros((3, WY, 128), jnp.float32)
    f0[1] = jnp.zeros((WX, WY, 128), jnp.float32)
    t1[1] = jnp.zeros((WX, WY, 128), jnp.float32)
    vals[...] = jnp.zeros_like(vals)
    bk[...] = jnp.zeros_like(bk)
    for axis in range(3):
        vals[axis, 2:10, 8:24] = STEP * cot[axis]

    def paint_back(plane, carry):
        totals = gathered(plane, 3)
        for q in range(3):
            for k in range(3):
                bk[3 * q + k, plane + 2, 8:32, :] = totals[q][k]
        return carry

    lax.fori_loop(0, BX + 2, paint_back, 0)

    def spread_back(plane, carry):
        at = plane + 1

        def cross(k):
            return 0.5 * (
                bk[k, at + 1, 8:32, :] - bk[k, at - 1, 8:32, :]
                + bk[3 + k, at, 9:33, :] - bk[3 + k, at, 7:31, :]
            )

        up = [0.5 * bk[6 + k, at, 8:32, :] for k in range(3)]
        parts = {
            -2: up[0],
            -1: cross(0) + up[1],
            1: cross(2) - up[1],
            2: -up[2],
        }
        main = cross(1) + up[2] - up[0]
        spill = None
        for step, value in parts.items():
            rolled = pltpu.roll(value, step % 128, 1)
            keep = lane >= step if step > 0 else lane < 128 + step
            main = main + jnp.where(keep, rolled, 0.0)
            over = jnp.where(keep, 0.0, rolled)
            spill = over if spill is None else spill + over
        f0[1, plane + 2] = main
        t1[1, plane + 2] = spill
        return carry

    lax.fori_loop(0, BX + 4, spread_back, 0)

    def pack(plane, carry):
        by = 8 * plane + 4
        out = []
        for q in range(2):
            out.append(carry[2 * q] + pltpu.roll(jnp.where(edge, f0[q, plane], 0.0), by, 1))
            out.append(carry[2 * q + 1] + pltpu.roll(t1[q, plane], by, 1))
        return tuple(out)

    empty = jnp.zeros((WY, 128), jnp.float32)
    packed = lax.fori_loop(2, BX + 6, pack, (empty,) * 4)
    for q in range(2):
        face, spill = packed[2 * q], packed[2 * q + 1]
        tsend[0, q] = jnp.where(upper, spill, face)
        tsend[1, q] = jnp.where(upper, face, spill)
        hp[q] = spill
    t_copies = [
        send(tsend.at[0], trecv.at[0], s_h.at[0], r_h.at[0], "gx", 1),
        send(tsend.at[1], trecv.at[1], s_h.at[1], r_h.at[1], "gx", ngx - 1),
    ]
    started += t_copies

    for copy in z_copies:
        copy.wait_recv()
    total = zbuf[c]
    for d in range(1, ngx):
        total = total + zrecv[d]
    loads["yt"].wait()
    ybuf[...] = dot(local["yt"][...], total).reshape(ngz, 48, 128)
    y_copies = [
        send(ybuf.at[lax.rem(b + d, ngz)], yrec.at[d], s_y.at[d], r_y.at[d], "gz", d)
        for d in range(1, ngz)
    ]
    started += y_copies

    for copy in t_copies:
        copy.wait_recv()
    fixes = []
    for q in range(2):
        from_left, from_right = trecv[0, q], trecv[1, q]
        hp[q] = hp[q] + jnp.where(upper, from_right, from_left)
        fixes.append(jnp.where(upper, from_left, from_right))

    def fix(plane, carry):
        by = 124 - 8 * plane
        by = jnp.where(by < 0, by + 128, by)
        for q in range(2):
            f0[q, plane] = f0[q, plane] + jnp.where(edge, pltpu.roll(fixes[q], by, 1), 0.0)
        return carry

    lax.fori_loop(2, BX + 6, fix, 0)
    rim_copies = [
        send(f0.at[:, 2:14, 16:24], yrecv.at[0], s_h.at[2], r_h.at[2], "gz", 1),
        send(f0.at[:, 2:14, 0:8], yrecv.at[1], s_h.at[3], r_h.at[3], "gz", ngz - 1),
        send(hp.at[:, 16:24], yhrecv.at[0], s_h.at[4], r_h.at[4], "gz", 1),
        send(hp.at[:, 0:8], yhrecv.at[1], s_h.at[5], r_h.at[5], "gz", ngz - 1),
    ]

    for copy in y_copies:
        copy.wait_recv()
    total = ybuf[b]
    for d in range(1, ngz):
        total = total + yrec[d]
    xrec[a] = total
    x_copies = [
        send(xrec.at[a], xrec.at[a], s_x.at[d], r_x.at[d], "gy", d) for d in range(1, ngy)
    ]
    started += x_copies

    for copy in rim_copies:
        copy.wait()
    f0[:, 2:14, 0:8] = f0[:, 2:14, 0:8] + yrecv[0]
    f0[:, 2:14, 16:24] = f0[:, 2:14, 16:24] + yrecv[1]
    hp[:, 0:8] = hp[:, 0:8] + yhrecv[0]
    hp[:, 16:24] = hp[:, 16:24] + yhrecv[1]
    loads["ka"].wait()
    loads["kb"].wait()
    squares = local["ka"][...] + local["kb"][0:1, :]
    zero = squares == 0.0
    gain = jnp.where(
        zero, 0.0, COUPLE * jnp.exp(-SPREAD * squares) / jnp.where(zero, 1.0, squares)
    )
    loads["xf"].wait()
    loads["xi"].wait()
    for copy in x_copies:
        copy.wait_recv()
    side_copies = [
        send(f0.at[0, 8:13], xrecv.at[0, 0], s_h.at[6], r_h.at[6], "gy", 1),
        send(f0.at[1, 9:14], xrecv.at[0, 1], s_h.at[7], r_h.at[7], "gy", 1),
        send(f0.at[0, 3:8], xrecv.at[1, 0], s_h.at[8], r_h.at[8], "gy", ngy - 1),
        send(f0.at[1, 2:7], xrecv.at[1, 1], s_h.at[9], r_h.at[9], "gy", ngy - 1),
        send(hp, xhrecv.at[0], s_h.at[10], r_h.at[10], "gy", 1),
        send(hp, xhrecv.at[1], s_h.at[11], r_h.at[11], "gy", ngy - 1),
    ]
    spectrum = dot(local["xf"][...], xrec[...].reshape(ngy * 48, 128))
    urec[b] = dot(local["xi"][...], gain * spectrum)
    u_copies = [
        send(urec.at[b], urec.at[b], s_u.at[d], r_u.at[d], "gz", d) for d in range(1, ngz)
    ]
    started += u_copies

    loads["yi"].wait()
    for copy in u_copies:
        copy.wait_recv()
    wrec[c] = dot(local["yi"][...], urec[...].reshape(ngz * 48, 128))
    w_copies = [
        send(wrec.at[c], wrec.at[c], s_w.at[d], r_w.at[d], "gx", d) for d in range(1, ngx)
    ]
    started += w_copies

    for copy in side_copies:
        copy.wait()
    f0[0, 0:5] = f0[0, 0:5] + xrecv[0, 0]
    f0[1, 1:6] = f0[1, 1:6] + xrecv[0, 1]
    f0[0, 11:16] = f0[0, 11:16] + xrecv[1, 0]
    f0[1, 10:15] = f0[1, 10:15] + xrecv[1, 1]
    rims = [
        hp[q]
        + jnp.where(
            lane < 64, pltpu.roll(xhrecv[0, q], 64, 1), pltpu.roll(xhrecv[1, q], 64, 1)
        )
        for q in range(2)
    ]

    def unpack(plane, carry):
        by = 124 - 8 * plane
        by = jnp.where(by < 0, by + 128, by)
        for q in range(2):
            t1[q, plane] = jnp.where(edge, pltpu.roll(rims[q], by, 1), 0.0)
        return carry

    lax.fori_loop(0, WX, unpack, 0)
    window = [
        jnp.concatenate([f0[q].reshape(WX * WY, 128), t1[q].reshape(WX * WY, 128)], axis=1)
        for q in range(2)
    ]
    loads["sz"].wait()
    loads["an"].wait()

    column = lax.broadcasted_iota(jnp.int32, (inner * WY, 128), 1)

    def keep(target, slot, value):
        own, past = value[:, 0:128], value[:, 128:256]
        before = jnp.where(column == 0, pltpu.roll(past, 1, 1), pltpu.roll(own, 1, 1))
        after = jnp.where(column == 127, pltpu.roll(past, 127, 1), pltpu.roll(own, 127, 1))
        for k, shifted in enumerate((before, own, after)):
            target[slot, k] = shifted.reshape(inner, WY, 128)

    smoothed = rdot(window[0], local["sz"][:, 0:256])
    keep(near, 0, dot(local["an"][0], smoothed))
    keep(near, 1, dot(local["an"][1], smoothed))
    keep(near, 2, dot(local["an"][2], rdot(window[0], local["sz"][:, 256:512])))
    keep(near, 3, -2.0 * dot(local["an"][2], rdot(window[1], local["sz"][:, 0:256])))

    def slopes(plane):
        rows = pl.ds(8, BY)
        weights = [wt[n, plane + 2, rows, :] for n in range(9)]
        slope = []
        for axis in range(3):
            shift = SMAX * bent[axis, plane]
            slope += [shift - 0.5, -2.0 * shift, shift + 0.5]
        return weights, slope

    def plus(total, term):
        return term if total is None else total + term

    even_row = lax.rem(lax.broadcasted_iota(jnp.int32, (BY, 128), 0), 2) == 0
    even_lane = lax.rem(lax.broadcasted_iota(jnp.int32, (BY, 128), 1), 2) == 0

    def read(plane, carry):
        weights, slope = slopes(plane)
        pushes = [vals[axis, plane + 2, 8:24, :] for axis in range(3)]
        sums = [None] * 6
        for k in range(3):
            mid = [None] * 6
            for j in range(3):
                line = [None] * 5
                for i in range(3):
                    at = [near[q, k, plane + i, pl.ds(j, BY), :] for q in range(4)]
                    both = at[3]
                    for q in range(3):
                        line[q] = plus(line[q], weights[i] * at[q])
                        both = both + pushes[q] * at[q]
                    line[3] = plus(line[3], weights[i] * both)
                    line[4] = plus(line[4], slope[i] * both)
                for q in range(3):
                    mid[q] = plus(mid[q], weights[3 + j] * line[q])
                mid[3] = plus(mid[3], weights[3 + j] * line[4])
                mid[4] = plus(mid[4], slope[3 + j] * line[3])
                mid[5] = plus(mid[5], weights[3 + j] * line[3])
            for q in range(5):
                sums[q] = plus(sums[q], weights[6 + k] * mid[q])
            sums[5] = plus(sums[5], slope[6 + k] * mid[5])
        for q in range(6):
            part[q, plane] = sums[q]
        even = (lax.rem(plane, 2) == 0, even_row, even_lane)
        for axis in range(3):
            for n, (low, mid, high) in enumerate(
                (weights[3 * axis : 3 * axis + 3], slope[3 * axis : 3 * axis + 3])
            ):
                cell[4 * axis + 2 * n, plane] = mid + jnp.where(even[axis], high, low)
                cell[4 * axis + 2 * n + 1, plane] = jnp.where(even[axis], low, high)
        return carry

    lax.fori_loop(0, BX, read, 0)

    for name in ("zi", "uf", "up"):
        loads[name].wait()
    for copy in w_copies:
        copy.wait_recv()
    spread = rdot(jnp.concatenate([wrec[d] for d in range(ngx)], axis=1), local["zi"][...])
    value, slant = spread[:, 0:128], spread[:, 128:256]
    far = [
        dot(local["uf"][0], value),
        dot(local["uf"][1], value),
        dot(local["uf"][2], slant),
    ]
    fine = dot(local["up"][...], spread[:, 256:512])
    for k in range(2):
        psi[k] = fine[:, 128 * k : 128 * (k + 1)].reshape(4, BX, BY, 128)
    for axis in range(3):
        moved[axis] = SMAX * bent[axis] + STEP * (
            part[axis] + far[axis].reshape(BX, BY, 128)
        )

    def finish(plane, carry):
        sums = [part[3 + axis, plane] for axis in range(3)]
        group = [cell[n, plane] for n in range(12)]
        for k in range(2):
            mid = [None] * 3
            for j in range(2):
                here, there = psi[k, j, plane], psi[k, 2 + j, plane]
                line = group[0] * here + group[1] * there
                tilt = group[2] * here + group[3] * there
                mid[0] = plus(mid[0], group[4 + j] * tilt)
                mid[1] = plus(mid[1], group[6 + j] * line)
                mid[2] = plus(mid[2], group[4 + j] * line)
            sums[0] = sums[0] + group[8 + k] * mid[0]
            sums[1] = sums[1] + group[8 + k] * mid[1]
            sums[2] = sums[2] + group[10 + k] * mid[2]
        for axis in range(3):
            bend = bent[axis, plane]
            grad[axis, plane] = (cot[axis, plane] + sums[axis]) * (SMAX * (1.0 - bend * bend))
        return carry

    lax.fori_loop(0, BX, finish, 0)
    for copy in started:
        copy.wait_send()


def body(tables, sizes, latent, cotangent):
    ngx, ngy, ngz = sizes
    dma = pltpu.SemaphoreType.DMA
    f32 = jnp.float32

    def vmem(*shape):
        return pltpu.VMEM(shape, f32)

    arrays = [jnp.asarray(tables[name]) for name in NAMES]
    locals_ = [
        pltpu.VMEM(array.shape[1:], array.dtype)
        for array in arrays
    ]
    scratch = [
        vmem(3, BX, BY, 128),
        vmem(3, BX, BY, 128),
        vmem(12, BX, BY, 128),
        vmem(3, BX, BY, 128),
        vmem(9, 12, 32, 128),
        vmem(3, 12, 32, 128),
        vmem(9, 14, 40, 128),
        vmem(2, WX, WY, 128),
        vmem(2, WX, WY, 128),
        vmem(2, WY, 128),
        vmem(2, 2, WY, 128),
        vmem(2, 2, WY, 128),
        vmem(2, 2, 12, 8, 128),
        vmem(2, 2, 8, 128),
        vmem(2, 2, 5, WY, 128),
        vmem(2, 2, WY, 128),
        vmem(ngx, 64, 128),
        vmem(ngx, 64, 128),
        vmem(ngz, 48, 128),
        vmem(ngz, 48, 128),
        vmem(ngy, 48, 128),
        vmem(ngz, 48, 128),
        vmem(ngx, 64, 128),
        vmem(4, 3, BX + 2, WY, 128),
        vmem(2, 4, BX, BY, 128),
        vmem(6, BX, BY, 128),
        dma((len(NAMES),)),
        dma((2,)),
        dma((ngx,)), dma((ngx,)),
        dma((ngz,)), dma((ngz,)),
        dma((ngz,)), dma((ngz,)),
        dma((ngx,)), dma((ngx,)),
        dma((ngy,)), dma((ngy,)),
        dma((12,)), dma((12,)),
    ]
    whole = pl.BlockSpec(memory_space=pltpu.VMEM)
    return pl.pallas_call(
        functools.partial(kernel, sizes),
        out_shape=[jax.ShapeDtypeStruct((3, BX, BY, BZ), f32)] * 2,
        in_specs=[pl.BlockSpec(memory_space=pl.ANY)] * (2 + len(NAMES)),
        out_specs=[whole, whole],
        scratch_shapes=locals_ + scratch,
        compiler_params=pltpu.CompilerParams(
            collective_id=0, has_side_effects=True, vmem_limit_bytes=54784 * 1024
        ),
    )(latent, cotangent, *arrays)


def solution(mesh):
    sizes = (mesh.shape["gx"], mesh.shape["gy"], mesh.shape["gz"])
    tables = make_tables(*sizes)
    placed = P(None, "gy", "gz", "gx")
    return jax.shard_map(
        functools.partial(body, tables, sizes),
        mesh=mesh,
        in_specs=(placed, placed),
        out_specs=(placed, placed),
        check_vma=False,
    )
```

```python
import functools
import math

import jax
import jax.numpy as jnp
import ml_dtypes
import numpy as np
from jax import lax
from jax.experimental import pallas as pl
from jax.experimental.pallas import tpu as pltpu
from jax.sharding import PartitionSpec as P

SMAX = 0.45
STEP = 0.5
SHORT = 4.0
COUPLE = 0.5
SPREAD = 0.125
KERNEL = (0.05, 0.25, 0.4, 0.25, 0.05)
MESH = pl.DeviceIdType.MESH

BX, BY, BZ = 8, 16, 128
CX, CY, CZ = 4, 8, 64
WX, WY = 16, 24


def basis(length):
    n = np.arange(length)
    angle = 2.0 * np.pi * ((n[:, None] * n[None, :]) % length) / length
    return (np.cos(angle) + np.sin(angle)) / math.sqrt(length)


def five(delta):
    return np.where(np.abs(delta) <= 2, np.take(np.array(KERNEL), np.clip(delta + 2, 0, 4)), 0.0)


def same(left, right):
    return (left[:, None] == right[None, :]).astype(np.float64)


def central(left, right):
    return 0.5 * (same(left + 1, right) - same(left - 1, right))


def make_tables(ngx, ngy, ngz):
    mx, my, mz = CX * ngy, CY * ngz, CZ * ngx
    qx, qy, qz = basis(mx), basis(my), basis(mz)
    f = {}
    cxe, cye = np.arange(-1, CX + 1), np.arange(-1, CY + 1)
    fx, fy = np.arange(-1, BX + 1), np.arange(-4, BY + 4)
    ox, oy, oz = np.arange(BX), np.arange(BY), np.arange(BZ)
    down = lambda v: np.floor_divide(v, 2)

    def rows64(matrix):
        return np.concatenate([matrix, np.zeros((64 - matrix.shape[0], matrix.shape[1]))])

    f["cd"] = rows64(np.kron(same(cxe, down(fx)), same(cye, down(fy)) * ((fy >= -1) & (fy <= BY))))
    own_x, own_y = same(cxe, down(ox)), same(cye, down(oy))
    f["cp"] = rows64(
        np.concatenate(
            [
                np.kron(-central(cxe, down(ox)), own_y),
                np.kron(own_x, -central(cye, down(oy))),
                np.kron(own_x, own_y),
            ],
            axis=1,
        )
    )
    zt = np.zeros((ngx, 512, ngx, 2, CZ))
    for c in range(ngx):
        zc = CZ * c + down(oz)
        q = qz.reshape(mz, ngx, CZ)
        zt[c, 0:128, :, 0] = q[zc % mz]
        zt[c, 128, :, 0] = q[(CZ * c + CZ) % mz]
        zt[c, 255, :, 0] = q[(CZ * c - 1) % mz]
        zt[c, 256:384, :, 1] = q[zc % mz]
        zt[c, 384:512, :, 1] = 0.5 * (q[(zc + 1) % mz] - q[(zc - 1) % mz])
    f["zt"] = zt.reshape(ngx, 512, ngx * 128)
    yt = np.zeros((ngz, ngz, 6, CY, 64))
    for b in range(ngz):
        for x in range(6):
            for y in range(10):
                yt[b, :, x, :, x * 10 + y] = qy[(CY * b + y - 1) % my].reshape(ngz, CY)
    f["yt"] = yt.reshape(ngz, ngz * 48, 64)
    xf = np.zeros((mx, CY, ngy, 6, CY))
    xi = np.zeros((ngy, 6, CY, mx, CY))
    for a in range(ngy):
        for x in range(6):
            for m in range(CY):
                xf[:, m, a, x, m] = qx[(CX * a + x - 1) % mx]
                xi[a, x, m, :, m] = qx[(CX * a + x - 1) % mx]
    f["xf"] = xf.reshape(mx * CY, ngy * 48)
    f["xi"] = xi.reshape(ngy, 48, mx * CY)
    square = lambda total: 4.0 * np.sin(np.pi * np.arange(total) / total) ** 2
    ka = square(mx)[None, :, None] + square(my).reshape(ngz, 1, CY)
    f["ka"] = np.broadcast_to(ka.reshape(ngz, mx * CY, 1), (ngz, mx * CY, 128))
    kb = np.concatenate([square(mz).reshape(ngx, CZ)] * 2, axis=1)
    f["kb"] = np.broadcast_to(kb[:, None], (ngx, 8, 128))
    yi = np.zeros((ngz, 64, ngz, 6, CY))
    for b in range(ngz):
        for x in range(6):
            for y in range(10):
                yi[b, x * 10 + y, :, x, :] = qy[(CY * b + y - 1) % my].reshape(ngz, CY)
    f["yi"] = yi.reshape(ngz, 64, ngz * 48)
    beside = lambda node: down(node) + np.where(node % 2 == 0, -1, 1)
    zi = np.zeros((ngx, ngx, 2, CZ, 512))
    for c in range(ngx):
        at = lambda cell: qz[(CZ * c + cell) % mz].T.reshape(ngx, CZ, 128)
        zi[c, :, 0, :, 0:128] = at(down(oz))
        zi[c, :, 0, :, 128:256] = 0.5 * (at(down(oz) + 1) - at(down(oz) - 1))
        zi[c, :, 1, :, 256:384] = at(down(oz))
        zi[c, :, 1, :, 384:512] = at(beside(oz))
    f["zi"] = zi.reshape(ngx, ngx * 128, 512)
    pad4 = lambda matrix: np.concatenate([matrix, np.zeros((matrix.shape[0], 4))], axis=1)
    f["uf"] = np.stack(
        [
            pad4(np.kron(central(down(ox), cxe), same(down(oy), cye))),
            pad4(np.kron(same(down(ox), cxe), central(down(oy), cye))),
            pad4(np.kron(same(down(ox), cxe), same(down(oy), cye))),
        ]
    )
    ry = np.arange(-1, WY - 1)
    row = ((ry <= BY) * 1.0)[:, None]
    cells = (down, beside)
    f["up"] = pad4(
        np.concatenate(
            [np.kron(same(p(ox), cxe), same(q(oy), cye)) for p in cells for q in cells]
        )
    )
    zw = np.concatenate([oz, oz + 128])
    zw[252:256] = np.arange(-4, 0)
    valid = np.concatenate([np.ones(128), np.ones(4), np.zeros(120), np.ones(4)])[:, None]
    tap = lambda target, extra: five(target[None, :] + extra - zw[:, None]) * valid
    own, past = oz, np.where(oz == 0, BZ, -1)
    ends = np.logical_or(oz == 0, oz == BZ - 1)[None, :]
    f["sz"] = np.concatenate(
        [tap(own, 0), tap(past, 0) * ends]
        + [tap(own, 1) - tap(own, -1), (tap(past, 1) - tap(past, -1)) * ends],
        axis=1,
    )
    wx, wy = np.arange(-4, WX - 4), np.arange(-4, WY - 4)
    kx = lambda extra: five(fx[:, None] + extra - wx[None, :])
    ky = lambda extra: five(ry[:, None] + extra - wy[None, :]) * row
    half = 0.5 * SHORT
    f["an"] = np.stack(
        [
            half * np.kron(kx(1) - kx(-1), ky(0)),
            half * np.kron(kx(0), ky(1) - ky(-1)),
            half * np.kron(kx(0), ky(0)),
        ]
    )
    f["cq"], f["c0"] = f["cp"][:, 0:256], f.pop("cp")[:, 256:384]
    tables = {}
    for name, value in f.items():
        if name not in AXIS_OF:
            value = value[None]
        value = value.astype(np.float32)
        if name in LEFT or name in RIGHT:
            high = value.astype(ml_dtypes.bfloat16)
            low = (value - high.astype(np.float32)).astype(ml_dtypes.bfloat16)
            value = np.concatenate([high, high, low], axis=-1 if name in LEFT else -2)
        least = -(-TABLE_BYTES // value[0].nbytes)
        filler = np.zeros((max(0, least - len(value)),) + value.shape[1:], value.dtype)
        tables[name] = np.ascontiguousarray(np.concatenate([value, filler]))
    return tables


TABLE_BYTES = 2**21
NAMES = (
    "cd", "cq", "c0", "zt", "yt", "xf", "xi", "ka", "kb", "yi", "sz", "an", "zi", "uf", "up",
)
LEFT = ("cd", "cq", "c0", "yt", "xf", "xi", "yi", "uf", "up", "an")
RIGHT = ("zt", "zi", "sz")


def halves(value):
    high = value.astype(jnp.bfloat16)
    low = (value - high.astype(jnp.float32)).astype(jnp.bfloat16)
    return high, low


def dot(table, value):
    high, low = halves(value)
    stacked = jnp.concatenate([high, low, high], axis=0)
    return jnp.dot(table, stacked, preferred_element_type=jnp.float32)


def rdot(value, table):
    high, low = halves(value)
    stacked = jnp.concatenate([high, low, high], axis=1)
    return jnp.dot(stacked, table, preferred_element_type=jnp.float32)


AXIS_OF = {"zt": "gx", "yt": "gz", "xi": "gy", "ka": "gz", "kb": "gx", "yi": "gz", "zi": "gx"}


def kernel(sizes, lat_hbm, cot_hbm, *refs):
    ngx, ngy, ngz = sizes
    tables = dict(zip(NAMES, refs[: len(NAMES)]))
    moved, grad = refs[len(NAMES) : len(NAMES) + 2]
    rest = refs[len(NAMES) + 2 :]
    local = dict(zip(NAMES, rest[: len(NAMES)]))
    (
        lat, cot, cell, bent, wt, vals, bk, f0, t1, hp, tsend, trecv, yrecv, yhrecv, xrecv, xhrecv,
        zbuf, zrecv, ybuf, yrec, xrec, urec, wrec, near, psi, part,
        table_sem, arg_sem, s_z, r_z, s_y, r_y, s_u, r_u, s_w, r_w, s_x, r_x, s_h, r_h,
    ) = rest[len(NAMES) :]
    c, a, b = lax.axis_index("gx"), lax.axis_index("gy"), lax.axis_index("gz")
    place = {"gx": c, "gy": a, "gz": b}
    size = {"gx": ngx, "gy": ngy, "gz": ngz}

    def other(axis, step):
        return {axis: lax.rem(place[axis] + step, size[axis])}

    arguments = [
        pltpu.make_async_copy(lat_hbm, lat, arg_sem.at[0]),
        pltpu.make_async_copy(cot_hbm, cot, arg_sem.at[1]),
    ]
    for copy in arguments:
        copy.start()
    barrier = pltpu.get_barrier_semaphore()
    partners = [(axis, step) for axis in size for step in range(1, size[axis])]
    for axis, step in partners:
        pl.semaphore_signal(barrier, inc=1, device_id=other(axis, step), device_id_type=MESH)
    loads = {}
    for number, name in enumerate(NAMES):
        source = tables[name].at[place[AXIS_OF[name]] if name in AXIS_OF else 0]
        loads[name] = pltpu.make_async_copy(source, local[name], table_sem.at[number])
        loads[name].start()

    started = []

    def send(source, target, send_sem, recv_sem, axis, step):
        copy = pltpu.make_async_remote_copy(
            src_ref=source,
            dst_ref=target,
            send_sem=send_sem,
            recv_sem=recv_sem,
            device_id=other(axis, step),
            device_id_type=MESH,
        )
        copy.start()
        return copy

    lane = lax.broadcasted_iota(jnp.int32, (WY, 128), 1)
    edge = jnp.logical_or(lane < 4, lane >= 124)
    upper = lax.rem(lane, 8) >= 4

    wt[...] = jnp.zeros_like(wt)
    arguments[0].wait()
    for axis in range(3):
        bend = jnp.tanh(lat[axis])
        bent[axis] = bend
        shift = SMAX * bend
        wt[3 * axis, 2:10, 8:24] = 0.5 * (0.5 - shift) ** 2
        wt[3 * axis + 1, 2:10, 8:24] = 0.75 - shift * shift
        wt[3 * axis + 2, 2:10, 8:24] = 0.5 * (0.5 + shift) ** 2

    def gathered(plane, charges):
        totals = [[None] * 3 for _ in range(charges or 1)]
        for i in range(3):
            at = plane + 2 - i
            for j in range(3):
                rows = pl.ds(5 - j, WY)
                cross = wt[i, at, rows, :] * wt[3 + j, at, rows, :]
                for k in range(3):
                    weight = cross * wt[6 + k, at, rows, :]
                    for q in range(charges or 1):
                        term = weight * vals[q, at, rows, :] if charges else weight
                        totals[q][k] = term if totals[q][k] is None else totals[q][k] + term
        return totals

    def paint(plane, carry):
        ((low, middle, high),) = gathered(plane, 0)
        low = pltpu.roll(low, 127, 1)
        high = pltpu.roll(high, 1, 1)
        keep_low, keep_high = lane < 127, lane >= 1
        main = middle + jnp.where(keep_low, low, 0.0) + jnp.where(keep_high, high, 0.0)
        spill = jnp.where(keep_low, 0.0, low) + jnp.where(keep_high, 0.0, high)
        f0[0, plane + 3] = main
        t1[0, plane + 3] = spill
        return carry

    lax.fori_loop(0, BX + 2, paint, 0, unroll=2)

    loads["cd"].wait()
    loads["cq"].wait()
    loads["c0"].wait()
    inner = BX + 2
    density = jnp.concatenate(
        [f0[0, 3:13].reshape(inner * WY, 128), t1[0, 3:13].reshape(inner * WY, 128)], axis=1
    )
    rho = dot(local["cd"][...], density)
    arguments[1].wait()
    pushed = [(STEP * cot[axis]).reshape(BX * BY, 128) for axis in range(3)]
    cross_source = dot(local["cq"][...], jnp.concatenate(pushed[:2], axis=0))
    along_source = dot(local["c0"][...], pushed[2])
    loads["zt"].wait()
    modes = rdot(jnp.concatenate([rho, cross_source, along_source], axis=1), local["zt"][...])
    for j in range(ngx):
        zbuf[j] = modes[:, 128 * j : 128 * (j + 1)]
    pl.semaphore_wait(barrier, len(partners))
    z_copies = [
        send(zbuf.at[lax.rem(c + d, ngx)], zrecv.at[d], s_z.at[d], r_z.at[d], "gx", d)
        for d in range(1, ngx)
    ]
    started += z_copies

    f0[0, 0:3] = jnp.zeros((3, WY, 128), jnp.float32)
    f0[0, 13:16] = jnp.zeros((3, WY, 128), jnp.float32)
    t1[0, 0:3] = jnp.zeros((3, WY, 128), jnp.float32)
    t1[0, 13:16] = jnp.zeros((3, WY, 128), jnp.float32)
    f0[1] = jnp.zeros((WX, WY, 128), jnp.float32)
    t1[1] = jnp.zeros((WX, WY, 128), jnp.float32)
    vals[...] = jnp.zeros_like(vals)
    bk[...] = jnp.zeros_like(bk)
    for axis in range(3):
        vals[axis, 2:10, 8:24] = STEP * cot[axis]

    def paint_back(plane, carry):
        totals = gathered(plane, 3)
        for q in range(3):
            for k in range(3):
                bk[3 * q + k, plane + 2, 8:32, :] = totals[q][k]
        return carry

    lax.fori_loop(0, BX + 2, paint_back, 0)

    def spread_back(plane, carry):
        at = plane + 1

        def cross(k):
            return 0.5 * (
                bk[k, at + 1, 8:32, :] - bk[k, at - 1, 8:32, :]
                + bk[3 + k, at, 9:33, :] - bk[3 + k, at, 7:31, :]
            )

        up = [0.5 * bk[6 + k, at, 8:32, :] for k in range(3)]
        parts = {
            -2: up[0],
            -1: cross(0) + up[1],
            1: cross(2) - up[1],
            2: -up[2],
        }
        main = cross(1) + up[2] - up[0]
        spill = None
        for step, value in parts.items():
            rolled = pltpu.roll(value, step % 128, 1)
            keep = lane >= step if step > 0 else lane < 128 + step
            main = main + jnp.where(keep, rolled, 0.0)
            over = jnp.where(keep, 0.0, rolled)
            spill = over if spill is None else spill + over
        f0[1, plane + 2] = main
        t1[1, plane + 2] = spill
        return carry

    lax.fori_loop(0, BX + 4, spread_back, 0)

    def pack(plane, carry):
        by = 8 * plane + 4
        out = []
        for q in range(2):
            out.append(carry[2 * q] + pltpu.roll(jnp.where(edge, f0[q, plane], 0.0), by, 1))
            out.append(carry[2 * q + 1] + pltpu.roll(t1[q, plane], by, 1))
        return tuple(out)

    empty = jnp.zeros((WY, 128), jnp.float32)
    packed = lax.fori_loop(2, BX + 6, pack, (empty,) * 4)
    for q in range(2):
        face, spill = packed[2 * q], packed[2 * q + 1]
        tsend[0, q] = jnp.where(upper, spill, face)
        tsend[1, q] = jnp.where(upper, face, spill)
        hp[q] = spill
    t_copies = [
        send(tsend.at[0], trecv.at[0], s_h.at[0], r_h.at[0], "gx", 1),
        send(tsend.at[1], trecv.at[1], s_h.at[1], r_h.at[1], "gx", ngx - 1),
    ]
    started += t_copies

    for copy in z_copies:
        copy.wait_recv()
    total = zbuf[c]
    for d in range(1, ngx):
        total = total + zrecv[d]
    loads["yt"].wait()
    ybuf[...] = dot(local["yt"][...], total).reshape(ngz, 48, 128)
    y_copies = [
        send(ybuf.at[lax.rem(b + d, ngz)], yrec.at[d], s_y.at[d], r_y.at[d], "gz", d)
        for d in range(1, ngz)
    ]
    started += y_copies

    for copy in t_copies:
        copy.wait_recv()
    fixes = []
    for q in range(2):
        from_left, from_right = trecv[0, q], trecv[1, q]
        hp[q] = hp[q] + jnp.where(upper, from_right, from_left)
        fixes.append(jnp.where(upper, from_left, from_right))

    def fix(plane, carry):
        by = 124 - 8 * plane
        by = jnp.where(by < 0, by + 128, by)
        for q in range(2):
            f0[q, plane] = f0[q, plane] + jnp.where(edge, pltpu.roll(fixes[q], by, 1), 0.0)
        return carry

    lax.fori_loop(2, BX + 6, fix, 0, unroll=2)
    rim_copies = [
        send(f0.at[:, 2:14, 16:24], yrecv.at[0], s_h.at[2], r_h.at[2], "gz", 1),
        send(f0.at[:, 2:14, 0:8], yrecv.at[1], s_h.at[3], r_h.at[3], "gz", ngz - 1),
        send(hp.at[:, 16:24], yhrecv.at[0], s_h.at[4], r_h.at[4], "gz", 1),
        send(hp.at[:, 0:8], yhrecv.at[1], s_h.at[5], r_h.at[5], "gz", ngz - 1),
    ]

    for copy in y_copies:
        copy.wait_recv()
    total = ybuf[b]
    for d in range(1, ngz):
        total = total + yrec[d]
    xrec[a] = total
    x_copies = [
        send(xrec.at[a], xrec.at[a], s_x.at[d], r_x.at[d], "gy", d) for d in range(1, ngy)
    ]
    started += x_copies

    for copy in rim_copies:
        copy.wait()
    f0[:, 2:14, 0:8] = f0[:, 2:14, 0:8] + yrecv[0]
    f0[:, 2:14, 16:24] = f0[:, 2:14, 16:24] + yrecv[1]
    hp[:, 0:8] = hp[:, 0:8] + yhrecv[0]
    hp[:, 16:24] = hp[:, 16:24] + yhrecv[1]
    loads["ka"].wait()
    loads["kb"].wait()
    squares = local["ka"][...] + local["kb"][0:1, :]
    zero = squares == 0.0
    gain = jnp.where(
        zero, 0.0, COUPLE * jnp.exp(-SPREAD * squares) / jnp.where(zero, 1.0, squares)
    )
    loads["xf"].wait()
    loads["xi"].wait()
    for copy in x_copies:
        copy.wait_recv()
    side_copies = [
        send(f0.at[0, 8:13], xrecv.at[0, 0], s_h.at[6], r_h.at[6], "gy", 1),
        send(f0.at[1, 9:14], xrecv.at[0, 1], s_h.at[7], r_h.at[7], "gy", 1),
        send(f0.at[0, 3:8], xrecv.at[1, 0], s_h.at[8], r_h.at[8], "gy", ngy - 1),
        send(f0.at[1, 2:7], xrecv.at[1, 1], s_h.at[9], r_h.at[9], "gy", ngy - 1),
        send(hp, xhrecv.at[0], s_h.at[10], r_h.at[10], "gy", 1),
        send(hp, xhrecv.at[1], s_h.at[11], r_h.at[11], "gy", ngy - 1),
    ]
    spectrum = dot(local["xf"][...], xrec[...].reshape(ngy * 48, 128))
    urec[b] = dot(local["xi"][...], gain * spectrum)
    u_copies = [
        send(urec.at[b], urec.at[b], s_u.at[d], r_u.at[d], "gz", d) for d in range(1, ngz)
    ]
    started += u_copies

    loads["yi"].wait()
    for copy in u_copies:
        copy.wait_recv()
    wrec[c] = dot(local["yi"][...], urec[...].reshape(ngz * 48, 128))
    w_copies = [
        send(wrec.at[c], wrec.at[c], s_w.at[d], r_w.at[d], "gx", d) for d in range(1, ngx)
    ]
    started += w_copies

    for copy in side_copies:
        copy.wait()
    f0[0, 0:5] = f0[0, 0:5] + xrecv[0, 0]
    f0[1, 1:6] = f0[1, 1:6] + xrecv[0, 1]
    f0[0, 11:16] = f0[0, 11:16] + xrecv[1, 0]
    f0[1, 10:15] = f0[1, 10:15] + xrecv[1, 1]
    rims = [
        hp[q]
        + jnp.where(
            lane < 64, pltpu.roll(xhrecv[0, q], 64, 1), pltpu.roll(xhrecv[1, q], 64, 1)
        )
        for q in range(2)
    ]

    def unpack(plane, carry):
        by = 124 - 8 * plane
        by = jnp.where(by < 0, by + 128, by)
        for q in range(2):
            t1[q, plane] = jnp.where(edge, pltpu.roll(rims[q], by, 1), 0.0)
        return carry

    lax.fori_loop(0, WX, unpack, 0, unroll=2)
    window = [
        jnp.concatenate([f0[q].reshape(WX * WY, 128), t1[q].reshape(WX * WY, 128)], axis=1)
        for q in range(2)
    ]
    loads["sz"].wait()
    loads["an"].wait()

    column = lax.broadcasted_iota(jnp.int32, (inner * WY, 128), 1)

    def keep(target, slot, value):
        own, past = value[:, 0:128], value[:, 128:256]
        before = jnp.where(column == 0, pltpu.roll(past, 1, 1), pltpu.roll(own, 1, 1))
        after = jnp.where(column == 127, pltpu.roll(past, 127, 1), pltpu.roll(own, 127, 1))
        for k, shifted in enumerate((before, own, after)):
            target[slot, k] = shifted.reshape(inner, WY, 128)

    smoothed = rdot(window[0], local["sz"][:, 0:256])
    keep(near, 0, dot(local["an"][0], smoothed))
    keep(near, 1, dot(local["an"][1], smoothed))
    keep(near, 2, dot(local["an"][2], rdot(window[0], local["sz"][:, 256:512])))
    keep(near, 3, -2.0 * dot(local["an"][2], rdot(window[1], local["sz"][:, 0:256])))

    def slopes(plane):
        rows = pl.ds(8, BY)
        weights = [wt[n, plane + 2, rows, :] for n in range(9)]
        slope = []
        for axis in range(3):
            shift = SMAX * bent[axis, plane]
            slope += [shift - 0.5, -2.0 * shift, shift + 0.5]
        return weights, slope

    def plus(total, term):
        return term if total is None else total + term

    even_row = lax.rem(lax.broadcasted_iota(jnp.int32, (BY, 128), 0), 2) == 0
    even_lane = lax.rem(lax.broadcasted_iota(jnp.int32, (BY, 128), 1), 2) == 0

    def read(plane, carry):
        weights, slope = slopes(plane)
        pushes = [vals[axis, plane + 2, 8:24, :] for axis in range(3)]
        sums = [None] * 6
        for k in range(3):
            mid = [None] * 6
            for j in range(3):
                line = [None] * 5
                for i in range(3):
                    at = [near[q, k, plane + i, pl.ds(j, BY), :] for q in range(4)]
                    both = at[3]
                    for q in range(3):
                        line[q] = plus(line[q], weights[i] * at[q])
                        both = both + pushes[q] * at[q]
                    line[3] = plus(line[3], weights[i] * both)
                    line[4] = plus(line[4], slope[i] * both)
                for q in range(3):
                    mid[q] = plus(mid[q], weights[3 + j] * line[q])
                mid[3] = plus(mid[3], weights[3 + j] * line[4])
                mid[4] = plus(mid[4], slope[3 + j] * line[3])
                mid[5] = plus(mid[5], weights[3 + j] * line[3])
            for q in range(5):
                sums[q] = plus(sums[q], weights[6 + k] * mid[q])
            sums[5] = plus(sums[5], slope[6 + k] * mid[5])
        for q in range(6):
            part[q, plane] = sums[q]
        even = (lax.rem(plane, 2) == 0, even_row, even_lane)
        for axis in range(3):
            for n, (low, mid, high) in enumerate(
                (weights[3 * axis : 3 * axis + 3], slope[3 * axis : 3 * axis + 3])
            ):
                cell[4 * axis + 2 * n, plane] = mid + jnp.where(even[axis], high, low)
                cell[4 * axis + 2 * n + 1, plane] = jnp.where(even[axis], low, high)
        return carry

    lax.fori_loop(0, BX, read, 0)

    for name in ("zi", "uf", "up"):
        loads[name].wait()
    for copy in w_copies:
        copy.wait_recv()
    spread = rdot(jnp.concatenate([wrec[d] for d in range(ngx)], axis=1), local["zi"][...])
    value, slant = spread[:, 0:128], spread[:, 128:256]
    far = [
        dot(local["uf"][0], value),
        dot(local["uf"][1], value),
        dot(local["uf"][2], slant),
    ]
    fine = dot(local["up"][...], spread[:, 256:512])
    for k in range(2):
        psi[k] = fine[:, 128 * k : 128 * (k + 1)].reshape(4, BX, BY, 128)
    for axis in range(3):
        moved[axis] = SMAX * bent[axis] + STEP * (
            part[axis] + far[axis].reshape(BX, BY, 128)
        )

    def finish(plane, carry):
        sums = [part[3 + axis, plane] for axis in range(3)]
        group = [cell[n, plane] for n in range(12)]
        for k in range(2):
            mid = [None] * 3
            for j in range(2):
                here, there = psi[k, j, plane], psi[k, 2 + j, plane]
                line = group[0] * here + group[1] * there
                tilt = group[2] * here + group[3] * there
                mid[0] = plus(mid[0], group[4 + j] * tilt)
                mid[1] = plus(mid[1], group[6 + j] * line)
                mid[2] = plus(mid[2], group[4 + j] * line)
            sums[0] = sums[0] + group[8 + k] * mid[0]
            sums[1] = sums[1] + group[8 + k] * mid[1]
            sums[2] = sums[2] + group[10 + k] * mid[2]
        for axis in range(3):
            bend = bent[axis, plane]
            grad[axis, plane] = (cot[axis, plane] + sums[axis]) * (SMAX * (1.0 - bend * bend))
        return carry

    lax.fori_loop(0, BX, finish, 0, unroll=2)
    for copy in started:
        copy.wait_send()


def body(tables, sizes, latent, cotangent):
    ngx, ngy, ngz = sizes
    dma = pltpu.SemaphoreType.DMA
    f32 = jnp.float32

    def vmem(*shape):
        return pltpu.VMEM(shape, f32)

    arrays = [jnp.asarray(tables[name]) for name in NAMES]
    locals_ = [
        pltpu.VMEM(array.shape[1:], array.dtype)
        for array in arrays
    ]
    scratch = [
        vmem(3, BX, BY, 128),
        vmem(3, BX, BY, 128),
        vmem(12, BX, BY, 128),
        vmem(3, BX, BY, 128),
        vmem(9, 12, 32, 128),
        vmem(3, 12, 32, 128),
        vmem(9, 14, 40, 128),
        vmem(2, WX, WY, 128),
        vmem(2, WX, WY, 128),
        vmem(2, WY, 128),
        vmem(2, 2, WY, 128),
        vmem(2, 2, WY, 128),
        vmem(2, 2, 12, 8, 128),
        vmem(2, 2, 8, 128),
        vmem(2, 2, 5, WY, 128),
        vmem(2, 2, WY, 128),
        vmem(ngx, 64, 128),
        vmem(ngx, 64, 128),
        vmem(ngz, 48, 128),
        vmem(ngz, 48, 128),
        vmem(ngy, 48, 128),
        vmem(ngz, 48, 128),
        vmem(ngx, 64, 128),
        vmem(4, 3, BX + 2, WY, 128),
        vmem(2, 4, BX, BY, 128),
        vmem(6, BX, BY, 128),
        dma((len(NAMES),)),
        dma((2,)),
        dma((ngx,)), dma((ngx,)),
        dma((ngz,)), dma((ngz,)),
        dma((ngz,)), dma((ngz,)),
        dma((ngx,)), dma((ngx,)),
        dma((ngy,)), dma((ngy,)),
        dma((12,)), dma((12,)),
    ]
    whole = pl.BlockSpec(memory_space=pltpu.VMEM)
    return pl.pallas_call(
        functools.partial(kernel, sizes),
        out_shape=[jax.ShapeDtypeStruct((3, BX, BY, BZ), f32)] * 2,
        in_specs=[pl.BlockSpec(memory_space=pl.ANY)] * (2 + len(NAMES)),
        out_specs=[whole, whole],
        scratch_shapes=locals_ + scratch,
        compiler_params=pltpu.CompilerParams(
            collective_id=0, has_side_effects=True, vmem_limit_bytes=54784 * 1024
        ),
    )(latent, cotangent, *arrays)


def solution(mesh):
    sizes = (mesh.shape["gx"], mesh.shape["gy"], mesh.shape["gz"])
    tables = make_tables(*sizes)
    placed = P(None, "gy", "gz", "gx")
    return jax.shard_map(
        functools.partial(body, tables, sizes),
        mesh=mesh,
        in_specs=(placed, placed),
        out_specs=(placed, placed),
        check_vma=False,
    )
```
